512 devices in a mesh: rows: 128 (over z_hi, x, y, core), cols: 4 (over z_lo).
Axes of the slice: x: 4, y: 4, z: 16 (z_hi: 4, z_lo: 4; z = z_hi * 4 + z_lo), core: 2. Of those that a mesh axis runs over, the one named last changes fastest.
Arguments:
- features: bfloat16 [8192, 512], P('rows', 'cols'), may hold values from -6 to 6
- weight: bfloat16 [512, 512], replicated, may hold values from -0.25 to 0.25
- cotangent: bfloat16 [32768, 512], P(('rows', 'cols')), may hold values from -6 to 6
- tile_slot: int32 [128, 32], P('rows'), may hold values from 0 to 127, as said below
- tile_count: int32 [128], P('rows'), may hold values from 8 to 32, as said below
- tile_edges: int32 [128, 32, 512], P('rows'), may hold values from 0 to 16383
- deg_dst: int32 [32768], P('rows'), may hold values from 0 to 1023
- deg_src: int32 [8192], P('rows'), may hold values from 0 to 1023
Outputs:
- activated: bfloat16 [32768, 512], P(('rows', 'cols'))
- weight_grad: float32 [512, 512], replicated
- feature_grad: bfloat16 [8192, 512], P('rows', 'cols')
The draws below stay inside these ranges and needn't reach their ends.
Inputs may be any that keep to these rules, and one draw needn't show every extreme that they name: `tile_slot`: within one row block the 32 slot numbers are distinct. Only the first tile_count[b] slots of row block b are in use; tile_slot and tile_edges of later slots are ignored.
All inputs are finite; a program needn't handle non-finite values.
Results may differ from the reference program's by a relative error of at most 0.0059.
Values may be sent and summed in bfloat16 or wider, within the bound.
No kernel may reach another device: no remote copies, remote signals or barrier semaphores. Data moves between devices by JAX's collectives and lax.ppermute only.
A program may use at most 64 MiB of HBM per device.

```python
import math
import jax
import jax.numpy as jnp
import numpy as np
from jax import lax

F = 512
TILE = 128
EPT = 512
NB = 256
BLOCKS = 128
NODES = 32768
SOURCES = 8192
TMAX = 32


def draw_tile_slot(key, part):
    key = jax.random.fold_in(key, 11)
    total_slots = NB // TILE * (SOURCES // TILE)
    key_list = jax.random.split(key, BLOCKS)
    orders = jax.vmap(lambda single: jax.random.permutation(single, total_slots))(key_list)
    chosen = jax.random.randint(jax.random.fold_in(key, 1), (), 0, BLOCKS)
    special = jnp.roll(jnp.arange(total_slots), 1)
    block_index = jnp.arange(BLOCKS)
    slot_rows = jnp.where(block_index[:, None] == chosen, special[None, :], orders)
    return slot_rows[:, :TMAX].astype(jnp.int32)


def draw_tile_count(key, part):
    key = jax.random.fold_in(key, 23)
    base_counts = jax.random.randint(key, (BLOCKS,), TMAX // 4, TMAX // 2 + 1)
    heavy = jax.random.randint(jax.random.fold_in(key, 1), (BLOCKS,), 0, 8) == 0
    first = jax.random.randint(jax.random.fold_in(key, 2), (), 0, BLOCKS)
    block_index = jnp.arange(BLOCKS)
    counts = jnp.where(heavy | (block_index == first), TMAX, base_counts)
    counts = jnp.where(block_index == (first + 1) % BLOCKS, TMAX // 4, counts)
    return counts.astype(jnp.int32)


def set_ends(drawn, rng, low, high):
    spot = [jax.random.randint(jax.random.fold_in(rng, axis), (), 0, length) for axis, length in enumerate(drawn.shape)]
    main_axis = drawn.shape.index(max(drawn.shape))
    next_to = spot[:main_axis] + [(spot[main_axis] + 1) % drawn.shape[main_axis]] + spot[main_axis + 1:]
    return drawn.at[tuple(spot)].set(low).at[tuple(next_to)].set(high)


def block_scale(rng, extent, cuts, smallest, top_value):
    def one(axis_at, blocks):
        draws = jax.random.uniform(jax.random.fold_in(jax.random.fold_in(rng, 6), axis_at), (blocks,), jnp.float32, smallest / len(cuts), top_value / len(cuts))
        return jnp.repeat(jnp.exp(draws), extent[axis_at] // blocks).reshape((-1,) + (1,) * (len(extent) - axis_at - 1))

    loudness = one(*cuts[0])
    for cut in cuts[1:]:
        loudness = loudness * one(*cut)
    return loudness


def rank_table(number_of, lean):
    portions = [(1 << 20) // math.isqrt(standing ** lean) + 1 for standing in range(1, number_of + 1)]
    deviation = 1 + sum(portions) // (1 << 30)
    return np.cumsum(np.array([max(1, weight // deviation) for weight in portions]))


def ranked(own_key, extent, number_of, skew):
    listing = rank_table(number_of, skew)
    pick = jax.random.randint(jax.random.fold_in(own_key, 1), extent, 0, int(listing[number_of - 1]))
    grade = jnp.searchsorted(jnp.asarray(listing, jnp.int32), pick, side="right")
    return jax.random.permutation(jax.random.fold_in(own_key, 2), number_of)[grade].astype(jnp.int32)


def scatter_about(own_key, shape, scale, most, cuts=(), dtype=jnp.bfloat16):
    factor_of = block_scale(own_key, shape, cuts, -0.22, 0.18) if cuts else 1.0
    values = jax.random.normal(own_key, shape, jnp.float32) * scale * factor_of
    return jnp.minimum(jnp.maximum(values, -most), most).astype(dtype)


def setup_inputs(seed: int = 0) -> dict:
    key_of = jax.random.split(jax.random.key(seed), 9)
    features = scatter_about(key_of[0], (SOURCES, F), 1.0, 6.0, ((0, 128), (1, 4)))
    weight = scatter_about(key_of[1], (F, F), F ** -0.5, 0.25)
    cotangent = scatter_about(key_of[2], (NODES, F), 1.0, 6.0, ((0, 512),))
    tile_slot = draw_tile_slot(jax.random.fold_in(key_of[8], 71), 0)
    tile_count = draw_tile_count(jax.random.fold_in(key_of[8], 71), 0)
    tile_edges = set_ends(jax.random.randint(key_of[5], (BLOCKS, TMAX, EPT), 0, TILE * TILE), jax.random.fold_in(key_of[5], 1), 0, (TILE * TILE) - 1).astype(jnp.int32)
    deg_dst = set_ends(ranked(key_of[6], (NODES,), 1024, 2), jax.random.fold_in(key_of[6], 3), 0, 1023).astype(jnp.int32)
    deg_src = set_ends(ranked(key_of[7], (SOURCES,), 1024, 2), jax.random.fold_in(key_of[7], 3), 0, 1023).astype(jnp.int32)
    return dict(features=features, weight=weight, cotangent=cotangent, tile_slot=tile_slot, tile_count=tile_count, tile_edges=tile_edges, deg_dst=deg_dst, deg_src=deg_src)


SQRT_TWO_PI = 0.7978845608028654
CUBIC = 0.044715

def gelu_parts(values):
    inner = SQRT_TWO_PI * (values + CUBIC * values * values * values)
    tanh_val = jnp.tanh(inner)
    output = 0.5 * values * (1.0 + tanh_val)
    slope = 0.5 * (1.0 + tanh_val) + 0.5 * values * (1.0 - tanh_val * tanh_val) * SQRT_TWO_PI * (1.0 + 3.0 * CUBIC * values * values)
    return (output, slope)

def reference(features, weight, cotangent, tile_slot, tile_count, tile_edges, deg_dst, deg_src):
    src_scale = lax.rsqrt(1.0 + deg_src.astype(jnp.float32))
    scaled = (features.astype(jnp.float32) * src_scale[:, None]).astype(jnp.bfloat16)
    col_tiles = SOURCES // TILE
    slot_index = jnp.arange(TMAX)

    def block_step(carry, entries):
        weight_acc, source_acc = carry
        slots, count, edges, degrees, cot_block = entries
        live_mask = (slot_index < count).astype(jnp.float32)
        row_ids = ((slots // col_tiles)[:, None] * TILE + edges // TILE).reshape(-1).astype(jnp.int32)
        col_ids = ((slots % col_tiles)[:, None] * TILE + edges % TILE).reshape(-1).astype(jnp.int32)
        edge_weight = jnp.broadcast_to(live_mask[:, None], edges.shape).reshape(-1)
        dst_scale = lax.rsqrt(1.0 + degrees.astype(jnp.float32))
        gathered = scaled[col_ids].astype(jnp.float32) * edge_weight[:, None]
        summed = jax.ops.segment_sum(gathered, row_ids, NB)
        aggregated = (summed * dst_scale[:, None]).astype(jnp.bfloat16)
        pre_act = jnp.dot(aggregated, weight, preferred_element_type=jnp.float32)
        output, slope = gelu_parts(pre_act)
        pre_grad = (cot_block.astype(jnp.float32) * slope).astype(jnp.bfloat16)
        weight_acc = weight_acc + jnp.dot(aggregated.T, pre_grad, preferred_element_type=jnp.float32)
        spread = jnp.dot(pre_grad, weight.T, preferred_element_type=jnp.float32)
        spread_grad = (spread * dst_scale[:, None]).astype(jnp.bfloat16)
        back_terms = spread_grad[row_ids].astype(jnp.float32) * edge_weight[:, None]
        source_acc = source_acc.at[col_ids].add(back_terms)
        return ((weight_acc, source_acc), output.astype(jnp.bfloat16))
    start = (jnp.zeros((F, F), jnp.float32), jnp.zeros((SOURCES, F), jnp.float32))
    inputs = (tile_slot, tile_count, tile_edges, deg_dst.reshape(BLOCKS, NB), cotangent.reshape(BLOCKS, NB, F))
    (weight_grad, source_acc), outputs = lax.scan(block_step, start, inputs)
    activated = outputs.reshape(NODES, F)
    feature_grad = (source_acc * src_scale[:, None]).astype(jnp.bfloat16)
    return (activated, weight_grad, feature_grad)
```

```python
import jax
import jax.numpy as jnp
from jax import lax
from jax.experimental import pallas as pl
from jax.experimental.pallas import tpu as pltpu
from jax.sharding import Mesh, PartitionSpec as P

TILE = 128
NB = 256
SUB = 64
SLOTS = 32
SQRT_TWO_PI = 0.7978845608028654
CUBIC = 0.044715
ROWS = ("zh", "x", "y", "c")
PLANE = ("x", "y", "c")
RING = ("zh", "zl")
FINE = (("zh", 4), ("x", 4), ("y", 4), ("c", 2), ("zl", 4))

VMEM = pl.BlockSpec(memory_space=pltpu.VMEM)
SMEM = pl.BlockSpec(memory_space=pltpu.SMEM)


def call(kernel, out_shape, in_specs, scratch=(), micros=2, name=None):
    single = not isinstance(out_shape, (tuple, list))
    return pl.pallas_call(
        kernel,
        out_shape=out_shape,
        in_specs=in_specs,
        out_specs=VMEM if single else [VMEM] * len(out_shape),
        scratch_shapes=list(scratch),
        compiler_params=pltpu.CompilerParams(vmem_limit_bytes=24 * 1024 * 1024),
        cost_estimate=pl.CostEstimate(
            flops=int(micros * 1e9), bytes_accessed=int(micros * 1e6), transcendentals=0
        ),
        name=name,
    )


def gelu_parts(values):
    inner = SQRT_TWO_PI * (values + CUBIC * values * values * values)
    tanh_val = jnp.tanh(inner)
    output = 0.5 * values * (1.0 + tanh_val)
    slope = 0.5 * (1.0 + tanh_val) + 0.5 * values * (1.0 - tanh_val * tanh_val) * SQRT_TWO_PI * (
        1.0 + 3.0 * CUBIC * values * values
    )
    return (output, slope)


def column(row):
    n = row.shape[1]
    first = lax.broadcasted_iota(jnp.int32, (n, n), 0)
    second = lax.broadcasted_iota(jnp.int32, (n, n), 1)
    return jnp.sum(jnp.where(first == second, row, 0.0), axis=1, keepdims=True)


def degree_scale(degrees):
    return column(lax.rsqrt(1.0 + degrees.astype(jnp.float32)))


def encode(edges):
    row = edges >> 7
    value = 1.0 + (edges & (TILE - 1)).astype(jnp.float32) * (1.0 / TILE)
    value = value * jnp.float32(2.0**-32)
    for bit in range(6):
        value = value * jnp.where(((row >> bit) & 1) == 1, jnp.float32(2.0 ** (1 << bit)), jnp.float32(1.0))
    return jnp.where(row >= SUB, -value, value)


def decode(values):
    values = values.astype(jnp.float32)
    rest = jnp.abs(values) * jnp.float32(2.0**32)
    row = jnp.where(values < 0.0, SUB, 0)
    for bit in range(5, -1, -1):
        big = rest >= jnp.float32(2.0 ** (1 << bit))
        rest = jnp.where(big, rest * jnp.float32(2.0 ** -(1 << bit)), rest)
        row = row + jnp.where(big, 1 << bit, 0)
    col = ((rest - 1.0) * TILE).astype(jnp.int32)
    return jnp.where(values == 0.0, -1, row * TILE + col)


def onehots(code):
    row = code >> 7
    col = code & (TILE - 1)
    positions = lax.broadcasted_iota(jnp.int32, (TILE, code.shape[1]), 0)
    one = jnp.float32(1.0)
    zero = jnp.float32(0.0)
    return (
        jnp.where(positions == row, one, zero).astype(jnp.bfloat16),
        jnp.where(positions == col, one, zero).astype(jnp.bfloat16),
    )


def nt(left, right):
    return lax.dot_general(left, right, (((1,), (1,)), ((), ())), preferred_element_type=jnp.float32)


def prepare(count_ref, feature_ref, degree_ref, slot_ref, edge_ref, out_ref, scale_ref):
    scale = degree_scale(degree_ref[...])
    scale_ref[...] = scale
    scaled = (feature_ref[...].astype(jnp.float32) * scale).astype(jnp.bfloat16)
    count = count_ref[0]
    live = lax.broadcasted_iota(jnp.int32, edge_ref.shape, 0) < count
    codes = jnp.where(live, encode(edge_ref[...]), 0.0).astype(jnp.bfloat16)
    used = lax.broadcasted_iota(jnp.int32, (1, SLOTS), 1) < count
    slots = jnp.where(used, slot_ref[...], -1).astype(jnp.float32)
    slots = jnp.concatenate([slots, jnp.zeros((1, TILE - SLOTS), jnp.float32)], axis=1)
    slots = jnp.broadcast_to(slots, (16, TILE)).astype(jnp.bfloat16)
    for i in range(4):
        out_ref[i, 0:SUB, :] = scaled
        for p in range(4):
            out_ref[i, SUB + p * SLOTS:SUB + (p + 1) * SLOTS, :] = codes[:, p * TILE:(p + 1) * TILE]
        out_ref[i, 192:208, :] = slots


def build_forward(slot_ref, count_ref, edge_ref, wide_ref):
    wide_ref[...] = jnp.zeros_like(wide_ref)
    count = count_ref[0]

    def step(group, carry):
        for k in range(4):
            j = group * 4 + k
            row, col = onehots(jnp.where(j < count, edge_ref[pl.ds(j, 1), :], -1))
            tile = nt(row, col).astype(jnp.bfloat16)
            row_at = pl.multiple_of((slot_ref[j] >> 6) * TILE, TILE)
            wide_ref[pl.ds(row_at, TILE), pl.ds(pl.multiple_of(j * TILE, TILE), TILE)] = tile
        return carry

    lax.fori_loop(0, (count + 3) >> 2, step, 0)


def build_backward(slot_ref, quarter_ref, ring_ref, out_ref, list_ref, code_ref):
    out_ref[...] = jnp.zeros_like(out_ref)
    for i in range(4):
        code_ref[i * TILE:(i + 1) * TILE, :] = decode(ring_ref[i, SUB:192, :])
    quarter = quarter_ref[0]
    total = slot_ref.shape[0]

    def scan(i, n):
        slot = slot_ref[i]
        hit = jnp.logical_and(slot >= 0, ((slot & 63) >> 4) == quarter)

        @pl.when(hit)
        def _():
            for k in range(4):
                list_ref[n + k] = i

        return n + hit.astype(jnp.int32)

    found = lax.fori_loop(0, total, scan, 0)

    def step(group, carry):
        for k in range(4):
            i = list_ref[group * 4 + k]
            slot = slot_ref[i]
            block = i >> 5
            at = block * TILE + (i & 31)
            code = jnp.concatenate([code_ref[pl.ds(at + p * SLOTS, 1), :] for p in range(4)], axis=1)
            row, col = onehots(code)
            tile = nt(col, row).astype(jnp.bfloat16)
            at = pl.multiple_of((slot & 15) * TILE, TILE)
            lane = pl.multiple_of((block * 2 + (slot >> 6)) * TILE, TILE)
            out_ref[pl.ds(at, TILE), pl.ds(lane, TILE)] = tile
        return carry

    lax.fori_loop(0, (found + 3) >> 2, step, 0)


def aggregate(slot_ref, core_ref, wide_ref, own_ref, other_ref, degree_ref, out_ref, picked):
    core = core_ref[0]
    for j in range(SLOTS):
        tile = slot_ref[j] & 63
        at = pl.multiple_of(((tile & 15) * 4 + (tile >> 4)) * SUB, SUB)
        own_at = pl.multiple_of(j * TILE + core * SUB, SUB)
        other_at = pl.multiple_of(j * TILE + (1 - core) * SUB, SUB)
        picked[pl.ds(own_at, SUB), :] = own_ref[pl.ds(at, SUB), :]
        picked[pl.ds(other_at, SUB), :] = other_ref[pl.ds(at, SUB), :]
    total = jnp.dot(wide_ref[...], picked[...], preferred_element_type=jnp.float32)
    out_ref[...] = (total * degree_scale(degree_ref[...])).astype(jnp.bfloat16)


def dense(part_ref, panel_ref, weight_ref, cot_ref, degree_ref, act_ref, spread_ref, term_ref):
    scale = degree_scale(degree_ref[pl.ds(part_ref[0], 1), :])
    rows = jnp.concatenate([panel_ref[p] for p in range(4)], axis=1)
    pre_act = jnp.dot(rows, weight_ref[...], preferred_element_type=jnp.float32)
    output, slope = gelu_parts(pre_act)
    act_ref[...] = output.astype(jnp.bfloat16)
    pre_grad = (cot_ref[...].astype(jnp.float32) * slope).astype(jnp.bfloat16)
    spread = (nt(pre_grad, weight_ref[...]) * scale).astype(jnp.bfloat16)
    for p in range(4):
        spread_ref[p] = spread[:, p * TILE:(p + 1) * TILE]
    terms = lax.dot_general(rows, pre_grad, (((0,), (0,)), ((), ())), preferred_element_type=jnp.float32)
    term_ref[...] = terms.astype(jnp.bfloat16)


def pack_ring(part_ref, spread_ref, out_ref):
    total = part_ref[0].astype(jnp.float32)
    for s in range(1, part_ref.shape[0]):
        total = total + part_ref[s].astype(jnp.float32)
    total = total.astype(jnp.bfloat16)
    for i in range(16):
        p = i % 4
        out_ref[i, 0:SUB, :] = spread_ref[p]
        out_ref[i, SUB:SUB + 16, :] = total[:, p * TILE:(p + 1) * TILE]


def sum_ring(ring_ref, out_ref):
    total = jnp.zeros((16, TILE), jnp.float32)
    for i in range(16):
        total = total + ring_ref[i, SUB:SUB + 16, :].astype(jnp.float32)
    total = total.astype(jnp.bfloat16)
    for i in range(4):
        out_ref[i] = total


def spread_back(adj_ref, ring_ref, out_ref, grad):
    for i in range(16):
        grad[i * SUB:(i + 1) * SUB, :] = ring_ref[i, 0:SUB, :]
    for block in range(8):
        rows = adj_ref[block * 256:(block + 1) * 256, :]
        terms = jnp.dot(rows, grad[...], preferred_element_type=jnp.float32).astype(jnp.bfloat16)
        for k in range(4):
            out_ref[block * 4 + k] = terms[k * SUB:(k + 1) * SUB, :]


def finish(plane_ref, scale_ref, feature_ref, weight_ref):
    total = plane_ref[0, 0:SUB, :].astype(jnp.float32)
    for s in range(1, 32):
        total = total + plane_ref[s, 0:SUB, :].astype(jnp.float32)
    feature_ref[...] = (total * scale_ref[...]).astype(jnp.bfloat16)
    for s in range(32):
        for p in range(4):
            weight_ref[s * 16:(s + 1) * 16, p * TILE:(p + 1) * TILE] = plane_ref[
                s, SUB + p * 16:SUB + (p + 1) * 16, :
            ].astype(jnp.float32)


def local(features, weight, cotangent, tile_slot, tile_count, tile_edges, deg_dst, deg_src):
    bf16 = jnp.bfloat16
    shape = jax.ShapeDtypeStruct
    zh, core, zl = lax.axis_index("zh"), lax.axis_index("c"), lax.axis_index("zl")
    slots = jnp.clip(tile_slot, 0, 127)
    edges = tile_edges[0]

    piece, src_scale = call(
        prepare,
        (shape((4, 208, TILE), bf16), shape((SUB, 1), jnp.float32)),
        [SMEM, VMEM, VMEM, VMEM, VMEM],
        micros=1,
        name="prepare",
    )(tile_count, features, deg_src[None], slots, edges)
    piece = lax.all_to_all(piece, "zh", 0, 0)
    wide = call(build_forward, shape((NB, SLOTS * TILE), bf16), [SMEM, SMEM, VMEM], micros=6, name="build_forward")(
        slots[0], tile_count, edges
    )
    piece, wide = lax.optimization_barrier((piece, wide))

    plane_sources = lax.all_to_all(jnp.broadcast_to(piece[:, :SUB], (16, 4, SUB, TILE)), ("x", "y"), 0, 0)
    adjacent = call(
        build_backward,
        shape((2048, 1024), bf16),
        [SMEM, SMEM, VMEM],
        [pltpu.SMEM((4 * SLOTS + 8,), jnp.int32), pltpu.VMEM((4 * TILE, TILE), jnp.int32)],
        micros=6,
        name="build_backward",
    )(piece[:, 192, :SLOTS].astype(jnp.int32).reshape(4 * SLOTS), zh[None], piece)
    own_sources = plane_sources.reshape(64 * SUB, TILE)
    own_sources, adjacent = lax.optimization_barrier((own_sources, adjacent))
    other_sources = lax.ppermute(own_sources, "c", [(0, 1), (1, 0)])

    aggregated = call(
        aggregate,
        shape((NB, TILE), bf16),
        [SMEM, SMEM, VMEM, VMEM, VMEM, VMEM],
        [pltpu.VMEM((SLOTS * TILE, TILE), bf16)],
        name="aggregate",
    )(slots[0], core[None], wide, own_sources, other_sources, deg_dst[None])

    panels = lax.all_to_all(aggregated.reshape(4, SUB, TILE), "zl", 0, 0)
    activated, spread, terms = call(
        dense,
        (shape((SUB, 512), bf16), shape((4, SUB, TILE), bf16), shape((512, 512), bf16)),
        [SMEM] + [VMEM] * 4,
        name="dense",
    )(zl[None], panels, weight, cotangent, deg_dst.reshape(4, SUB))

    parts = lax.all_to_all(terms.reshape(32, 16, 512), PLANE, 0, 0)
    ring = call(pack_ring, shape((16, SUB + 16, TILE), bf16), [VMEM] * 2, name="pack_ring")(parts, spread)
    ring = lax.all_to_all(ring, RING, 0, 0)
    panel_sum = call(sum_ring, shape((4, 16, TILE), bf16), [VMEM], micros=1, name="sum_ring")(ring)
    weight_rows = lax.all_to_all(panel_sum, "zl", 0, 0).reshape(SUB, TILE)
    source_terms = call(
        spread_back,
        shape((32, SUB, TILE), bf16),
        [VMEM] * 2,
        [pltpu.VMEM((1024, TILE), bf16)],
        name="spread_back",
    )(adjacent, ring)
    plane = jnp.concatenate([source_terms, jnp.broadcast_to(weight_rows, (32, SUB, TILE))], axis=1)
    plane = lax.all_to_all(plane, PLANE, 0, 0)
    feature_grad, weight_grad = call(
        finish, (shape((SUB, TILE), bf16), shape((512, 512), jnp.float32)), [VMEM] * 2, name="finish"
    )(plane, src_scale)
    return (activated, weight_grad, feature_grad)


def solution(mesh):
    fine = Mesh(mesh.devices.reshape([size for _, size in FINE]), [name for name, _ in FINE])
    in_specs = (
        P(ROWS, "zl"),
        P(),
        P(ROWS + ("zl",), None),
        P(ROWS, None),
        P(ROWS),
        P(ROWS, None, None),
        P(ROWS),
        P(ROWS),
    )
    out_specs = (P(ROWS + ("zl",), None), P(), P(ROWS, "zl"))
    return jax.shard_map(local, mesh=fine, in_specs=in_specs, out_specs=out_specs, check_vma=False)
```

```python
import jax
import jax.numpy as jnp
from jax import lax
from jax.experimental import pallas as pl
from jax.experimental.pallas import tpu as pltpu
from jax.sharding import Mesh, PartitionSpec as P

TILE = 128
NB = 256
SUB = 64
SLOTS = 32
SQRT_TWO_PI = 0.7978845608028654
CUBIC = 0.044715
ROWS = ("zh", "x", "y", "c")
PLANE = ("x", "y", "c")
RING = ("zh", "zl")
FINE = (("zh", 4), ("x", 4), ("y", 4), ("c", 2), ("zl", 4))

VMEM = pl.BlockSpec(memory_space=pltpu.VMEM)
SMEM = pl.BlockSpec(memory_space=pltpu.SMEM)
HBM = pl.BlockSpec(memory_space=pltpu.HBM)


def call(kernel, out_shape, in_specs, scratch=(), micros=2, name=None, out_spec=VMEM, limit=24):
    single = not isinstance(out_shape, (tuple, list))
    return pl.pallas_call(
        kernel,
        out_shape=out_shape,
        in_specs=in_specs,
        out_specs=out_spec if single else [out_spec] * len(out_shape),
        scratch_shapes=list(scratch),
        compiler_params=pltpu.CompilerParams(vmem_limit_bytes=limit * 1024 * 1024),
        cost_estimate=pl.CostEstimate(
            flops=int(micros * 1e9), bytes_accessed=int(micros * 1e6), transcendentals=0
        ),
        name=name,
    )


def gelu_parts(values):
    inner = SQRT_TWO_PI * (values + CUBIC * values * values * values)
    tanh_val = jnp.tanh(inner)
    output = 0.5 * values * (1.0 + tanh_val)
    slope = 0.5 * (1.0 + tanh_val) + 0.5 * values * (1.0 - tanh_val * tanh_val) * SQRT_TWO_PI * (
        1.0 + 3.0 * CUBIC * values * values
    )
    return (output, slope)


def column(row):
    n = row.shape[1]
    first = lax.broadcasted_iota(jnp.int32, (n, n), 0)
    second = lax.broadcasted_iota(jnp.int32, (n, n), 1)
    return jnp.sum(jnp.where(first == second, row, 0.0), axis=1, keepdims=True)


def degree_scale(degrees):
    return column(lax.rsqrt(1.0 + degrees.astype(jnp.float32)))


def encode(edges):
    row = edges >> 7
    value = 1.0 + (edges & (TILE - 1)).astype(jnp.float32) * (1.0 / TILE)
    value = value * jnp.float32(2.0**-32)
    for bit in range(6):
        value = value * jnp.where(((row >> bit) & 1) == 1, jnp.float32(2.0 ** (1 << bit)), jnp.float32(1.0))
    return jnp.where(row >= SUB, -value, value)


def decode(values):
    values = values.astype(jnp.float32)
    rest = jnp.abs(values) * jnp.float32(2.0**32)
    row = jnp.where(values < 0.0, SUB, 0)
    for bit in range(5, -1, -1):
        big = rest >= jnp.float32(2.0 ** (1 << bit))
        rest = jnp.where(big, rest * jnp.float32(2.0 ** -(1 << bit)), rest)
        row = row + jnp.where(big, 1 << bit, 0)
    col = ((rest - 1.0) * TILE).astype(jnp.int32)
    return jnp.where(values == 0.0, -1, row * TILE + col)


def onehot(index):
    positions = lax.broadcasted_iota(jnp.int32, (TILE, index.shape[1]), 0)
    return jnp.where(positions == index, jnp.float32(1.0), jnp.float32(0.0)).astype(jnp.bfloat16)


def nt(left, right):
    return lax.dot_general(left, right, (((1,), (1,)), ((), ())), preferred_element_type=jnp.float32)


def start_copies(sems, *pairs):
    copies = [pltpu.make_async_copy(source, target, sems.at[i]) for i, (source, target) in enumerate(pairs)]
    for copy in copies:
        copy.start()
    return copies


def slot_row(count, slots):
    place = lax.broadcasted_iota(jnp.int32, (1, SLOTS), 1)
    rest = jnp.where(lax.broadcasted_iota(jnp.int32, (1, TILE - SLOTS), 1) == 0, count, 0)
    return jnp.concatenate([jnp.where(place < count, slots & 127, -1), rest], axis=1)


def prepare(count_ref, feature_hbm, degree_hbm, slot_hbm, edge_hbm, out_ref, scale_ref, feature, degree, slot, edge, sems):
    copies = start_copies(
        sems, (degree_hbm, degree), (feature_hbm, feature), (slot_hbm, slot), (edge_hbm.at[0], edge)
    )
    count = count_ref[0]
    copies[0].wait()
    scale = degree_scale(degree[...])
    scale_ref[...] = scale
    copies[1].wait()
    scaled = (feature[...].astype(jnp.float32) * scale).astype(jnp.bfloat16)
    copies[2].wait()
    slots = slot_row(count, slot[...])
    slots = jnp.broadcast_to(slots.astype(jnp.float32), (16, TILE)).astype(jnp.bfloat16)
    copies[3].wait()
    live = lax.broadcasted_iota(jnp.int32, edge.shape, 0) < count
    codes = jnp.where(live, encode(edge[...]), 0.0).astype(jnp.bfloat16)
    for i in range(4):
        out_ref[i, 0:SUB, :] = scaled
        for p in range(4):
            out_ref[i, SUB + p * SLOTS:SUB + (p + 1) * SLOTS, :] = codes[:, p * TILE:(p + 1) * TILE]
        out_ref[i, 192:208, :] = slots


def mark_edges(count_ref, slot_ref, edge_ref, code_ref):
    count = count_ref[0]
    row = jnp.broadcast_to(slot_row(count, slot_ref[...]), (8, TILE))
    code_ref[SLOTS:SLOTS + 8, :] = jnp.concatenate([row] * 4, axis=1)
    edges = edge_ref[0]
    live = lax.broadcasted_iota(jnp.int32, edges.shape, 0) < count
    code_ref[0:SLOTS, :] = jnp.where(live, edges, -1)


def build_forward(slot_ref, core_ref, code_ref, wide_ref):
    wide_ref[...] = jnp.zeros_like(wide_ref)
    first = core_ref[0] * SUB
    for b in range(2):

        def step(group, carry):
            for k in range(4):
                j = group * 4 + k
                code = code_ref[b, pl.ds(j, 1), :]
                col = (code & (TILE - 1)) - first
                col = jnp.where(jnp.logical_and(col >= 0, col < SUB), col + (k % 2) * SUB, -1)
                tile = nt(onehot(code >> 7), onehot(col)).astype(jnp.bfloat16)
                row_at = pl.multiple_of(((slot_ref[b, j] >> 6) & 1) * TILE, TILE)
                lane = pl.multiple_of((group * 2 + k // 2) * TILE, TILE)
                wide_ref[b, pl.ds(row_at, TILE), pl.ds(lane, TILE)] += tile
            return carry

        lax.fori_loop(0, (slot_ref[b, SLOTS] + 3) >> 2, step, 0)


def build_backward(slot_ref, quarter_ref, ring_ref, out_ref, list_ref, code_ref):
    out_ref[...] = jnp.zeros_like(out_ref)
    for i in range(4):
        code_ref[i * TILE:(i + 1) * TILE, :] = decode(ring_ref[i, SUB:192, :])
    quarter = quarter_ref[0]
    total = slot_ref.shape[0]

    def scan(i, n):
        slot = slot_ref[i]
        hit = jnp.logical_and(slot >= 0, ((slot & 63) >> 4) == quarter)

        @pl.when(hit)
        def _():
            for k in range(4):
                list_ref[n + k] = i

        return n + hit.astype(jnp.int32)

    found = lax.fori_loop(0, total, scan, 0)

    def step(group, carry):
        for k in range(4):
            i = list_ref[group * 4 + k]
            slot = slot_ref[i]
            block = i >> 5
            at = block * TILE + (i & 31)
            code = jnp.concatenate([code_ref[pl.ds(at + p * SLOTS, 1), :] for p in range(4)], axis=1)
            tile = nt(onehot(code & (TILE - 1)), onehot(code >> 7)).astype(jnp.bfloat16)
            at = pl.multiple_of((slot & 15) * TILE, TILE)
            lane = pl.multiple_of((block * 2 + (slot >> 6)) * TILE, TILE)
            out_ref[pl.ds(at, TILE), pl.ds(lane, TILE)] = tile
        return carry

    lax.fori_loop(0, (found + 3) >> 2, step, 0)


def aggregate(slot_ref, wide_ref, source_ref, out_ref, picked):
    for b in range(2):
        for j in range(SLOTS):
            tile = slot_ref[b, j] & 63
            at = pl.multiple_of(((tile & 15) * 4 + (tile >> 4)) * SUB, SUB)
            picked[b, j * SUB:(j + 1) * SUB, :] = source_ref[pl.ds(at, SUB), :]
        total = jnp.dot(wide_ref[b], picked[b], preferred_element_type=jnp.float32)
        for k in range(4):
            out_ref[b * 4 + k] = total[k * SUB:(k + 1) * SUB, :]


def dense(part_ref, panel_ref, weight_ref, cot_ref, degree_ref, act_ref, spread_ref, term_ref):
    scale = degree_scale(degree_ref[pl.ds(part_ref[0], 1), :])
    rows = jnp.concatenate(
        [((panel_ref[p] + panel_ref[p + 4]) * scale).astype(jnp.bfloat16) for p in range(4)], axis=1
    )
    pre_act = jnp.dot(rows, weight_ref[...], preferred_element_type=jnp.float32)
    output, slope = gelu_parts(pre_act)
    act_ref[...] = output.astype(jnp.bfloat16)
    pre_grad = (cot_ref[...].astype(jnp.float32) * slope).astype(jnp.bfloat16)
    spread = (nt(pre_grad, weight_ref[...]) * scale).astype(jnp.bfloat16)
    for p in range(4):
        spread_ref[p] = spread[:, p * TILE:(p + 1) * TILE]
    terms = lax.dot_general(rows, pre_grad, (((0,), (0,)), ((), ())), preferred_element_type=jnp.float32)
    term_ref[...] = terms.astype(jnp.bfloat16)


def pack_ring(part_ref, spread_ref, out_ref):
    total = part_ref[0].astype(jnp.float32)
    for s in range(1, part_ref.shape[0]):
        total = total + part_ref[s].astype(jnp.float32)
    total = total.astype(jnp.bfloat16)
    for i in range(16):
        p = i % 4
        out_ref[i, 0:SUB, :] = spread_ref[p]
        out_ref[i, SUB:SUB + 16, :] = total[:, p * TILE:(p + 1) * TILE]


def sum_ring(ring_ref, out_ref):
    total = jnp.zeros((16, TILE), jnp.float32)
    for i in range(16):
        total = total + ring_ref[i, SUB:SUB + 16, :].astype(jnp.float32)
    total = total.astype(jnp.bfloat16)
    for i in range(4):
        out_ref[i] = total


def spread_back(adj_ref, ring_ref, out_ref, grad):
    for i in range(16):
        grad[i * SUB:(i + 1) * SUB, :] = ring_ref[i, 0:SUB, :]
    for i in range(8):
        rows = adj_ref[i * 256:(i + 1) * 256, :]
        terms = jnp.dot(rows, grad[...], preferred_element_type=jnp.float32).astype(jnp.bfloat16)
        for k in range(4):
            out_ref[i * 4 + k] = terms[k * SUB:(k + 1) * SUB, :]


def finish(plane_ref, scale_ref, feature_ref, weight_ref):
    total = plane_ref[0, 0:SUB, :].astype(jnp.float32)
    for s in range(1, 32):
        total = total + plane_ref[s, 0:SUB, :].astype(jnp.float32)
    feature_ref[...] = (total * scale_ref[...]).astype(jnp.bfloat16)
    for s in range(32):
        for p in range(4):
            weight_ref[s * 16:(s + 1) * 16, p * TILE:(p + 1) * TILE] = plane_ref[
                s, SUB + p * 16:SUB + (p + 1) * 16, :
            ].astype(jnp.float32)


def local(features, weight, cotangent, tile_slot, tile_count, tile_edges, deg_dst, deg_src):
    bf16 = jnp.bfloat16
    shape = jax.ShapeDtypeStruct
    zh, core, zl = lax.axis_index("zh"), lax.axis_index("c"), lax.axis_index("zl")

    piece, src_scale = call(
        prepare,
        (shape((4, 208, TILE), bf16), shape((SUB, 1), jnp.float32)),
        [SMEM, HBM, HBM, HBM, HBM],
        [
            pltpu.VMEM((SUB, TILE), bf16),
            pltpu.VMEM((1, SUB), jnp.int32),
            pltpu.VMEM((1, SLOTS), jnp.int32),
            pltpu.VMEM((SLOTS, 512), jnp.int32),
            pltpu.SemaphoreType.DMA((4,)),
        ],
        micros=1,
        name="prepare",
        limit=62,
    )(tile_count, features, deg_src[None], tile_slot, tile_edges)
    code = call(
        mark_edges,
        shape((SLOTS + 8, 512), jnp.int32),
        [SMEM, VMEM, VMEM],
        micros=1,
        name="mark_edges",
    )(tile_count, tile_slot, tile_edges)
    ring_piece = lax.all_to_all(piece, "zh", 0, 0)
    codes = lax.all_gather(code, "c")
    slots = codes[:, SLOTS, :TILE]
    ring_piece, codes = lax.optimization_barrier((ring_piece, codes))

    plane_sources = lax.all_to_all(jnp.broadcast_to(ring_piece[:, :SUB], (16, 4, SUB, TILE)), ("x", "y"), 0, 0)
    wide = call(
        build_forward,
        shape((2, NB, SLOTS * SUB), bf16),
        [SMEM, SMEM, VMEM],
        micros=6,
        name="build_forward",
    )(slots, core[None], codes)
    plane_sources, wide = lax.optimization_barrier((plane_sources, wide))

    partial = call(
        aggregate,
        shape((8, SUB, TILE), jnp.float32),
        [SMEM, VMEM, VMEM],
        [pltpu.VMEM((2, SLOTS * SUB, TILE), bf16)],
        name="aggregate",
    )(slots, wide, plane_sources.reshape(64 * SUB, TILE))

    panels = lax.all_to_all(partial, ("c", "zl"), 0, 0)
    activated, spread, terms = call(
        dense,
        (shape((SUB, 512), bf16), shape((4, SUB, TILE), bf16), shape((512, 512), bf16)),
        [SMEM] + [VMEM] * 4,
        name="dense",
    )(zl[None], panels, weight, cotangent, deg_dst.reshape(4, SUB))

    parts = lax.all_to_all(terms.reshape(32, 16, 512), PLANE, 0, 0)
    ring = call(pack_ring, shape((16, SUB + 16, TILE), bf16), [VMEM] * 2, name="pack_ring")(parts, spread)
    ring = lax.all_to_all(ring, RING, 0, 0)
    adjacent = call(
        build_backward,
        shape((2048, 1024), bf16),
        [SMEM, SMEM, VMEM],
        [pltpu.SMEM((4 * SLOTS + 8,), jnp.int32), pltpu.VMEM((4 * TILE, TILE), jnp.int32)],
        micros=6,
        name="build_backward",
    )(ring_piece[:, 192, :SLOTS].astype(jnp.int32).reshape(4 * SLOTS), zh[None], ring_piece)
    ring, adjacent = lax.optimization_barrier((ring, adjacent))
    panel_sum = call(sum_ring, shape((4, 16, TILE), bf16), [VMEM], micros=1, name="sum_ring")(ring)
    weight_rows = lax.all_to_all(panel_sum, "zl", 0, 0).reshape(SUB, TILE)
    source_terms = call(
        spread_back,
        shape((32, SUB, TILE), bf16),
        [VMEM] * 2,
        [pltpu.VMEM((1024, TILE), bf16)],
        name="spread_back",
    )(adjacent, ring)
    plane = jnp.concatenate([source_terms, jnp.broadcast_to(weight_rows, (32, SUB, TILE))], axis=1)
    plane = lax.all_to_all(plane, PLANE, 0, 0)
    feature_grad, weight_grad = call(
        finish, (shape((SUB, TILE), bf16), shape((512, 512), jnp.float32)), [VMEM] * 2, name="finish"
    )(plane, src_scale)
    return (activated, weight_grad, feature_grad)


def solution(mesh):
    fine = Mesh(mesh.devices.reshape([size for _, size in FINE]), [name for name, _ in FINE])
    in_specs = (
        P(ROWS, "zl"),
        P(),
        P(ROWS + ("zl",), None),
        P(ROWS, None),
        P(ROWS),
        P(ROWS, None, None),
        P(ROWS),
        P(ROWS),
    )
    out_specs = (P(ROWS + ("zl",), None), P(), P(ROWS, "zl"))
    return jax.shard_map(local, mesh=fine, in_specs=in_specs, out_specs=out_specs, check_vma=False)
```

```python
import jax
import jax.numpy as jnp
from jax import lax
from jax.experimental import pallas as pl
from jax.experimental.pallas import tpu as pltpu
from jax.sharding import Mesh, PartitionSpec as P

TILE = 128
NB = 256
SUB = 64
SLOTS = 32
SQRT_TWO_PI = 0.7978845608028654
CUBIC = 0.044715
ROWS = ("zh", "x", "y", "c")
PLANE = ("x", "y", "c")
FINE = (("zh", 4), ("x", 4), ("y", 4), ("c", 2), ("zl", 4))

VMEM = pl.BlockSpec(memory_space=pltpu.VMEM)
SMEM = pl.BlockSpec(memory_space=pltpu.SMEM)
HBM = pl.BlockSpec(memory_space=pltpu.HBM)


def call(kernel, out_shape, in_specs, scratch=(), micros=2, name=None, out_spec=VMEM, limit=24):
    single = not isinstance(out_shape, (tuple, list))
    return pl.pallas_call(
        kernel,
        out_shape=out_shape,
        in_specs=in_specs,
        out_specs=out_spec if single else [out_spec] * len(out_shape),
        scratch_shapes=list(scratch),
        compiler_params=pltpu.CompilerParams(vmem_limit_bytes=limit * 1024 * 1024),
        cost_estimate=pl.CostEstimate(
            flops=int(micros * 1e9), bytes_accessed=int(micros * 1e6), transcendentals=0
        ),
        name=name,
    )


def gelu_parts(values):
    inner = SQRT_TWO_PI * (values + CUBIC * values * values * values)
    tanh_val = jnp.tanh(inner)
    output = 0.5 * values * (1.0 + tanh_val)
    slope = 0.5 * (1.0 + tanh_val) + 0.5 * values * (1.0 - tanh_val * tanh_val) * SQRT_TWO_PI * (
        1.0 + 3.0 * CUBIC * values * values
    )
    return (output, slope)


def column(row):
    n = row.shape[1]
    first = lax.broadcasted_iota(jnp.int32, (n, n), 0)
    second = lax.broadcasted_iota(jnp.int32, (n, n), 1)
    return jnp.sum(jnp.where(first == second, row, 0.0), axis=1, keepdims=True)


def degree_scale(degrees):
    return column(lax.rsqrt(1.0 + degrees.astype(jnp.float32)))


def encode(edges):
    row = edges >> 7
    value = 1.0 + (edges & (TILE - 1)).astype(jnp.float32) * (1.0 / TILE)
    value = value * jnp.float32(2.0**-32)
    for bit in range(6):
        value = value * jnp.where(((row >> bit) & 1) == 1, jnp.float32(2.0 ** (1 << bit)), jnp.float32(1.0))
    return jnp.where(row >= SUB, -value, value)


def decode(values):
    values = values.astype(jnp.float32)
    rest = jnp.abs(values) * jnp.float32(2.0**32)
    row = jnp.where(values < 0.0, SUB, 0)
    for bit in range(5, -1, -1):
        big = rest >= jnp.float32(2.0 ** (1 << bit))
        rest = jnp.where(big, rest * jnp.float32(2.0 ** -(1 << bit)), rest)
        row = row + jnp.where(big, 1 << bit, 0)
    col = ((rest - 1.0) * TILE).astype(jnp.int32)
    return jnp.where(values == 0.0, -1, row * TILE + col)


def onehot(index):
    positions = lax.broadcasted_iota(jnp.int32, (TILE, index.shape[1]), 0)
    return jnp.where(positions == index, jnp.float32(1.0), jnp.float32(0.0)).astype(jnp.bfloat16)


def nt(left, right):
    return lax.dot_general(left, right, (((1,), (1,)), ((), ())), preferred_element_type=jnp.float32)


def start_copies(sems, *pairs):
    copies = [pltpu.make_async_copy(source, target, sems.at[i]) for i, (source, target) in enumerate(pairs)]
    for copy in copies:
        copy.start()
    return copies


def slot_row(count, slots):
    place = lax.broadcasted_iota(jnp.int32, (1, SLOTS), 1)
    rest = jnp.where(lax.broadcasted_iota(jnp.int32, (1, TILE - SLOTS), 1) == 0, count, 0)
    return jnp.concatenate([jnp.where(place < count, slots & 127, -1), rest], axis=1)


def prepare(count_ref, feature_hbm, degree_hbm, slot_hbm, edge_hbm, out_ref, scale_ref, feature, degree, slot, edge, sems):
    copies = start_copies(
        sems, (degree_hbm, degree), (feature_hbm, feature), (slot_hbm, slot), (edge_hbm.at[0], edge)
    )
    count = count_ref[0]
    copies[0].wait()
    scale = degree_scale(degree[...])
    scale_ref[...] = scale
    copies[1].wait()
    scaled = (feature[...].astype(jnp.float32) * scale).astype(jnp.bfloat16)
    copies[2].wait()
    slots = slot_row(count, slot[...])
    slots = jnp.broadcast_to(slots.astype(jnp.float32), (16, TILE)).astype(jnp.bfloat16)
    copies[3].wait()
    live = lax.broadcasted_iota(jnp.int32, edge.shape, 0) < count
    codes = jnp.where(live, encode(edge[...]), 0.0).astype(jnp.bfloat16)
    out_ref[0:SUB, :] = scaled
    for p in range(4):
        out_ref[SUB + p * SLOTS:SUB + (p + 1) * SLOTS, :] = codes[:, p * TILE:(p + 1) * TILE]
    out_ref[192:208, :] = slots


def mark_edges(count_ref, slot_ref, edge_ref, code_ref):
    count = count_ref[0]
    row = jnp.broadcast_to(slot_row(count, slot_ref[...]), (8, TILE))
    code_ref[SLOTS:SLOTS + 8, :] = jnp.concatenate([row] * 4, axis=1)
    edges = edge_ref[0]
    live = lax.broadcasted_iota(jnp.int32, edges.shape, 0) < count
    code_ref[0:SLOTS, :] = jnp.where(live, edges, -1)


def build_forward(slot_ref, core_ref, code_ref, wide_ref):
    wide_ref[...] = jnp.zeros_like(wide_ref)
    first = core_ref[0] * SUB
    for b in range(2):

        def step(group, carry):
            for k in range(4):
                j = group * 4 + k
                code = code_ref[b, pl.ds(j, 1), :]
                col = (code & (TILE - 1)) - first
                col = jnp.where(jnp.logical_and(col >= 0, col < SUB), col + (k % 2) * SUB, -1)
                tile = nt(onehot(code >> 7), onehot(col)).astype(jnp.bfloat16)
                row_at = pl.multiple_of(((slot_ref[b, j] >> 6) & 1) * TILE, TILE)
                lane = pl.multiple_of((group * 2 + k // 2) * TILE, TILE)
                wide_ref[b, pl.ds(row_at, TILE), pl.ds(lane, TILE)] += tile
            return carry

        lax.fori_loop(0, (slot_ref[b, SLOTS] + 3) >> 2, step, 0)


def build_backward(slot_ref, quarter_ref, ring_ref, out_ref, list_ref, code_ref):
    out_ref[...] = jnp.zeros_like(out_ref)
    for i in range(4):
        code_ref[i * TILE:(i + 1) * TILE, :] = decode(ring_ref[i, SUB:192, :])
    quarter = quarter_ref[0]
    total = slot_ref.shape[0]

    def scan(i, n):
        slot = slot_ref[i]
        hit = jnp.logical_and(slot >= 0, ((slot & 63) >> 4) == quarter)

        @pl.when(hit)
        def _():
            for k in range(4):
                list_ref[n + k] = i

        return n + hit.astype(jnp.int32)

    found = lax.fori_loop(0, total, scan, 0)

    def step(group, carry):
        for k in range(4):
            i = list_ref[group * 4 + k]
            slot = slot_ref[i]
            block = i >> 5
            at = block * TILE + (i & 31)
            code = jnp.concatenate([code_ref[pl.ds(at + p * SLOTS, 1), :] for p in range(4)], axis=1)
            tile = nt(onehot(code & (TILE - 1)), onehot(code >> 7)).astype(jnp.bfloat16)
            at = pl.multiple_of((slot & 15) * TILE, TILE)
            lane = pl.multiple_of((block * 2 + (slot >> 6)) * TILE, TILE)
            out_ref[pl.ds(at, TILE), pl.ds(lane, TILE)] = tile
        return carry

    lax.fori_loop(0, (found + 3) >> 2, step, 0)


def aggregate(slot_ref, wide_ref, source_ref, out_ref, picked):
    for b in range(2):
        for j in range(SLOTS):
            tile = slot_ref[b, j] & 63
            at = pl.multiple_of(((tile & 15) * 4 + (tile >> 4)) * SUB, SUB)
            picked[b, j * SUB:(j + 1) * SUB, :] = source_ref[pl.ds(at, SUB), :]
        total = jnp.dot(wide_ref[b], picked[b], preferred_element_type=jnp.float32)
        for k in range(4):
            out_ref[b * 4 + k] = total[k * SUB:(k + 1) * SUB, :]


def dense(part_ref, panel_ref, weight_ref, cot_ref, degree_ref, act_ref, spread_ref, term_ref):
    scale = degree_scale(degree_ref[pl.ds(part_ref[0], 1), :])
    rows = jnp.concatenate(
        [((panel_ref[p] + panel_ref[p + 4]) * scale).astype(jnp.bfloat16) for p in range(4)], axis=1
    )
    pre_act = jnp.dot(rows, weight_ref[...], preferred_element_type=jnp.float32)
    output, slope = gelu_parts(pre_act)
    act_ref[...] = output.astype(jnp.bfloat16)
    pre_grad = (cot_ref[...].astype(jnp.float32) * slope).astype(jnp.bfloat16)
    spread = (nt(pre_grad, weight_ref[...]) * scale).astype(jnp.bfloat16)
    for p in range(4):
        spread_ref[p] = spread[:, p * TILE:(p + 1) * TILE]
    terms = lax.dot_general(rows, pre_grad, (((0,), (0,)), ((), ())), preferred_element_type=jnp.float32)
    term_ref[...] = terms.astype(jnp.bfloat16)


def sum_first(ref, first=0, last=None):
    total = ref[0, first:last].astype(jnp.float32)
    for s in range(1, ref.shape[0]):
        total = total + ref[s, first:last].astype(jnp.float32)
    return total.astype(jnp.bfloat16)


def pack_panels(part_ref, spread_ref, out_ref):
    total = sum_first(part_ref)
    piece = jnp.concatenate([total[:, p * TILE:(p + 1) * TILE] for p in range(4)], axis=0)
    for p in range(4):
        out_ref[p, 0:SUB, :] = spread_ref[p]
        out_ref[p, SUB:TILE, :] = piece


def merge_panels(panel_ref, out_ref):
    for i in range(4):
        out_ref[i * SUB:(i + 1) * SUB, :] = panel_ref[i, 0:SUB, :]
    out_ref[NB:NB + SUB, :] = sum_first(panel_ref, SUB, TILE)


def spread_back(adj_ref, ring_ref, out_ref, grad):
    for i in range(4):
        grad[i * NB:(i + 1) * NB, :] = ring_ref[i, 0:NB, :]
    piece = sum_first(ring_ref, NB, NB + SUB)
    for i in range(8):
        rows = adj_ref[i * 256:(i + 1) * 256, :]
        terms = jnp.dot(rows, grad[...], preferred_element_type=jnp.float32).astype(jnp.bfloat16)
        for k in range(4):
            out_ref[i * 4 + k, 0:SUB, :] = terms[k * SUB:(k + 1) * SUB, :]
            out_ref[i * 4 + k, SUB:TILE, :] = piece


def finish(plane_ref, scale_ref, feature_ref, weight_ref):
    total = plane_ref[0, 0:SUB, :].astype(jnp.float32)
    for s in range(1, 32):
        total = total + plane_ref[s, 0:SUB, :].astype(jnp.float32)
    feature_ref[...] = (total * scale_ref[...]).astype(jnp.bfloat16)
    for s in range(32):
        for p in range(4):
            weight_ref[s * 16:(s + 1) * 16, p * TILE:(p + 1) * TILE] = plane_ref[
                s, SUB + p * 16:SUB + (p + 1) * 16, :
            ].astype(jnp.float32)


def local(features, weight, cotangent, tile_slot, tile_count, tile_edges, deg_dst, deg_src):
    bf16 = jnp.bfloat16
    shape = jax.ShapeDtypeStruct
    zh, core, zl = lax.axis_index("zh"), lax.axis_index("c"), lax.axis_index("zl")

    piece, src_scale = call(
        prepare,
        (shape((208, TILE), bf16), shape((SUB, 1), jnp.float32)),
        [SMEM, HBM, HBM, HBM, HBM],
        [
            pltpu.VMEM((SUB, TILE), bf16),
            pltpu.VMEM((1, SUB), jnp.int32),
            pltpu.VMEM((1, SLOTS), jnp.int32),
            pltpu.VMEM((SLOTS, 512), jnp.int32),
            pltpu.SemaphoreType.DMA((4,)),
        ],
        micros=1,
        name="prepare",
        limit=62,
    )(tile_count, features, deg_src[None], tile_slot, tile_edges)
    code = call(
        mark_edges,
        shape((SLOTS + 8, 512), jnp.int32),
        [SMEM, VMEM, VMEM],
        micros=1,
        name="mark_edges",
    )(tile_count, tile_slot, tile_edges)
    ring_piece = lax.all_gather(piece, "zh")
    codes = lax.all_gather(code, "c")
    slots = codes[:, SLOTS, :TILE]

    plane_sources = lax.all_to_all(jnp.broadcast_to(ring_piece[:, :SUB], (16, 4, SUB, TILE)), ("x", "y"), 0, 0)
    wide = call(
        build_forward,
        shape((2, NB, SLOTS * SUB), bf16),
        [SMEM, SMEM, VMEM],
        micros=6,
        name="build_forward",
    )(slots, core[None], codes)
    plane_sources, wide = lax.optimization_barrier((plane_sources, wide))

    partial = call(
        aggregate,
        shape((8, SUB, TILE), jnp.float32),
        [SMEM, VMEM, VMEM],
        [pltpu.VMEM((2, SLOTS * SUB, TILE), bf16)],
        name="aggregate",
    )(slots, wide, plane_sources.reshape(64 * SUB, TILE))

    panels = lax.all_to_all(partial, ("c", "zl"), 0, 0)
    activated, spread, terms = call(
        dense,
        (shape((SUB, 512), bf16), shape((4, SUB, TILE), bf16), shape((512, 512), bf16)),
        [SMEM] + [VMEM] * 4,
        name="dense",
    )(zl[None], panels, weight, cotangent, deg_dst.reshape(4, SUB))

    parts = lax.all_to_all(terms.reshape(32, 16, 512), PLANE, 0, 0)
    adjacent = call(
        build_backward,
        shape((2048, 1024), bf16),
        [SMEM, SMEM, VMEM],
        [pltpu.SMEM((4 * SLOTS + 8,), jnp.int32), pltpu.VMEM((4 * TILE, TILE), jnp.int32)],
        micros=6,
        name="build_backward",
    )(ring_piece[:, 192, :SLOTS].astype(jnp.int32).reshape(4 * SLOTS), zh[None], ring_piece)
    parts, adjacent = lax.optimization_barrier((parts, adjacent))
    panels = call(pack_panels, shape((4, TILE, TILE), bf16), [VMEM] * 2, micros=1, name="pack_panels")(parts, spread)
    panels = lax.all_to_all(panels, "zl", 0, 0)
    merged = call(merge_panels, shape((NB + SUB, TILE), bf16), [VMEM], micros=1, name="merge_panels")(panels)
    ring = lax.all_gather(merged, "zh")
    plane = call(
        spread_back,
        shape((32, TILE, TILE), bf16),
        [VMEM] * 2,
        [pltpu.VMEM((1024, TILE), bf16)],
        name="spread_back",
    )(adjacent, ring)
    plane = lax.all_to_all(plane, PLANE, 0, 0)
    feature_grad, weight_grad = call(
        finish, (shape((SUB, TILE), bf16), shape((512, 512), jnp.float32)), [VMEM] * 2, name="finish"
    )(plane, src_scale)
    return (activated, weight_grad, feature_grad)


def solution(mesh):
    fine = Mesh(mesh.devices.reshape([size for _, size in FINE]), [name for name, _ in FINE])
    in_specs = (
        P(ROWS, "zl"),
        P(),
        P(ROWS + ("zl",), None),
        P(ROWS, None),
        P(ROWS),
        P(ROWS, None, None),
        P(ROWS),
        P(ROWS),
    )
    out_specs = (P(ROWS + ("zl",), None), P(), P(ROWS, "zl"))
    return jax.shard_map(local, mesh=fine, in_specs=in_specs, out_specs=out_specs, check_vma=False)
```

```python
import jax
import jax.numpy as jnp
from jax import lax
from jax.experimental import pallas as pl
from jax.experimental.pallas import tpu as pltpu
from jax.sharding import Mesh, PartitionSpec as P

TILE = 128
NB = 256
SUB = 64
SLOTS = 32
SQRT_TWO_PI = 0.7978845608028654
CUBIC = 0.044715
ROWS = ("zh", "x", "y", "c")
PLANE = ("x", "y", "c")
FINE = (("zh", 4), ("x", 4), ("y", 4), ("c", 2), ("zl", 4))

VMEM = pl.BlockSpec(memory_space=pltpu.VMEM)
SMEM = pl.BlockSpec(memory_space=pltpu.SMEM)
HBM = pl.BlockSpec(memory_space=pltpu.HBM)


def call(kernel, out_shape, in_specs, scratch=(), micros=2, name=None, out_spec=VMEM, limit=24):
    single = not isinstance(out_shape, (tuple, list))
    return pl.pallas_call(
        kernel,
        out_shape=out_shape,
        in_specs=in_specs,
        out_specs=out_spec if single else [out_spec] * len(out_shape),
        scratch_shapes=list(scratch),
        compiler_params=pltpu.CompilerParams(vmem_limit_bytes=limit * 1024 * 1024),
        cost_estimate=pl.CostEstimate(
            flops=int(micros * 1e9), bytes_accessed=int(micros * 1e6), transcendentals=0
        ),
        name=name,
    )


def gelu_parts(values):
    inner = SQRT_TWO_PI * (values + CUBIC * values * values * values)
    tanh_val = jnp.tanh(inner)
    output = 0.5 * values * (1.0 + tanh_val)
    slope = 0.5 * (1.0 + tanh_val) + 0.5 * values * (1.0 - tanh_val * tanh_val) * SQRT_TWO_PI * (
        1.0 + 3.0 * CUBIC * values * values
    )
    return (output, slope)


def column(row):
    n = row.shape[1]
    first = lax.broadcasted_iota(jnp.int32, (n, n), 0)
    second = lax.broadcasted_iota(jnp.int32, (n, n), 1)
    return jnp.sum(jnp.where(first == second, row, 0.0), axis=1, keepdims=True)


def degree_scale(degrees):
    return column(lax.rsqrt(1.0 + degrees.astype(jnp.float32)))


def encode(edges):
    row = edges >> 7
    value = 1.0 + (edges & (TILE - 1)).astype(jnp.float32) * (1.0 / TILE)
    value = value * jnp.float32(2.0**-32)
    for bit in range(6):
        value = value * jnp.where(((row >> bit) & 1) == 1, jnp.float32(2.0 ** (1 << bit)), jnp.float32(1.0))
    return jnp.where(row >= SUB, -value, value)


def decode(values):
    values = values.astype(jnp.float32)
    rest = jnp.abs(values) * jnp.float32(2.0**32)
    row = jnp.where(values < 0.0, SUB, 0)
    for bit in range(5, -1, -1):
        big = rest >= jnp.float32(2.0 ** (1 << bit))
        rest = jnp.where(big, rest * jnp.float32(2.0 ** -(1 << bit)), rest)
        row = row + jnp.where(big, 1 << bit, 0)
    col = ((rest - 1.0) * TILE).astype(jnp.int32)
    return jnp.where(values == 0.0, -1, row * TILE + col)


def onehot(index, rows=TILE):
    positions = lax.broadcasted_iota(jnp.int32, (rows, index.shape[1]), 0)
    return jnp.where(positions == index, jnp.float32(1.0), jnp.float32(0.0)).astype(jnp.bfloat16)


def nt(left, right):
    return lax.dot_general(left, right, (((1,), (1,)), ((), ())), preferred_element_type=jnp.float32)


def start_copies(sems, *pairs):
    copies = [pltpu.make_async_copy(source, target, sems.at[i]) for i, (source, target) in enumerate(pairs)]
    for copy in copies:
        copy.start()
    return copies


def slot_row(count, slots):
    place = lax.broadcasted_iota(jnp.int32, (1, SLOTS), 1)
    rest = jnp.where(lax.broadcasted_iota(jnp.int32, (1, TILE - SLOTS), 1) == 0, count, 0)
    return jnp.concatenate([jnp.where(place < count, slots & 127, -1), rest], axis=1)


def prepare(count_ref, feature_hbm, degree_hbm, slot_hbm, edge_hbm, out_ref, scale_ref, feature, degree, slot, edge, sems):
    copies = start_copies(
        sems, (degree_hbm, degree), (feature_hbm, feature), (slot_hbm, slot), (edge_hbm.at[0], edge)
    )
    count = count_ref[0]
    copies[0].wait()
    scale = degree_scale(degree[...])
    scale_ref[...] = scale
    copies[1].wait()
    scaled = (feature[...].astype(jnp.float32) * scale).astype(jnp.bfloat16)
    copies[2].wait()
    slots = slot_row(count, slot[...])
    slots = jnp.broadcast_to(slots.astype(jnp.float32), (16, TILE)).astype(jnp.bfloat16)
    copies[3].wait()
    live = lax.broadcasted_iota(jnp.int32, edge.shape, 0) < count
    codes = jnp.where(live, encode(edge[...]), 0.0).astype(jnp.bfloat16)
    out_ref[0:SUB, :] = scaled
    for p in range(4):
        out_ref[SUB + p * SLOTS:SUB + (p + 1) * SLOTS, :] = codes[:, p * TILE:(p + 1) * TILE]
    out_ref[192:208, :] = slots


def mark_edges(count_ref, slot_ref, edge_ref, code_ref):
    count = count_ref[0]
    row = jnp.broadcast_to(slot_row(count, slot_ref[...]), (8, TILE))
    code_ref[SLOTS:SLOTS + 8, :] = jnp.concatenate([row] * 4, axis=1)
    edges = edge_ref[0]
    live = lax.broadcasted_iota(jnp.int32, edges.shape, 0) < count
    code_ref[0:SLOTS, :] = jnp.where(live, edges, -1)


def build_forward(slot_ref, core_ref, code_ref, degree_ref, tiles_ref, scale_ref):
    scale_ref[...] = degree_scale(degree_ref[...])
    tiles_ref[...] = jnp.zeros_like(tiles_ref)
    first = core_ref[0] * SUB
    for b in range(2):

        def step(group, carry):
            for k in range(2):
                pair = []
                for parity in range(2):
                    code = code_ref[b, pl.ds(group * 4 + k * 2 + parity, 1), :]
                    row = onehot(code >> 7)
                    pair.append(nt(row, onehot((code & (TILE - 1)) - first, SUB)))
                lane = pl.multiple_of((group * 2 + k) * TILE, TILE)
                tiles_ref[b, :, pl.ds(lane, TILE)] = jnp.concatenate(pair, axis=1).astype(jnp.bfloat16)
            return carry

        lax.fori_loop(0, (slot_ref[b, SLOTS] + 3) >> 2, step, 0)


def build_backward(slot_ref, quarter_ref, ring_ref, out_ref, list_ref, code_ref):
    out_ref[...] = jnp.zeros_like(out_ref)
    for i in range(4):
        code_ref[i * TILE:(i + 1) * TILE, :] = decode(ring_ref[i, SUB:192, :])
    quarter = quarter_ref[0]
    total = slot_ref.shape[0]

    def scan(i, n):
        slot = slot_ref[i]
        hit = jnp.logical_and(slot >= 0, ((slot & 63) >> 4) == quarter)

        @pl.when(hit)
        def _():
            for k in range(4):
                list_ref[n + k] = i

        return n + hit.astype(jnp.int32)

    found = lax.fori_loop(0, total, scan, 0)

    def step(group, carry):
        for k in range(4):
            i = list_ref[group * 4 + k]
            slot = slot_ref[i]
            block = i >> 5
            at = block * TILE + (i & 31)
            code = jnp.concatenate([code_ref[pl.ds(at + p * SLOTS, 1), :] for p in range(4)], axis=1)
            tile = nt(onehot(code & (TILE - 1)), onehot(code >> 7)).astype(jnp.bfloat16)
            at = pl.multiple_of((slot & 15) * TILE, TILE)
            lane = pl.multiple_of((block * 2 + (slot >> 6)) * TILE, TILE)
            out_ref[pl.ds(at, TILE), pl.ds(lane, TILE)] = tile
        return carry

    lax.fori_loop(0, (found + 3) >> 2, step, 0)


def aggregate(slot_ref, core_ref, tiles_ref, source_ref, own_ref, other_ref, picked):
    core = core_ref[0]
    for b in range(2):
        picked[b] = jnp.zeros((SLOTS * SUB, 2 * TILE), jnp.bfloat16)
        for j in range(SLOTS):
            slot = slot_ref[b, j]
            tile = slot & 63
            at = pl.multiple_of(((tile & 15) * 4 + (tile >> 4)) * SUB, SUB)
            lane = pl.multiple_of(((slot >> 6) & 1) * TILE, TILE)
            picked[b, j * SUB:(j + 1) * SUB, pl.ds(lane, TILE)] = source_ref[pl.ds(at, SUB), :]
        total = jnp.dot(tiles_ref[b], picked[b], preferred_element_type=jnp.float32)
        for group in range(2):
            part = total[:, group * TILE:(group + 1) * TILE]

            @pl.when(core == b)
            def _():
                own_ref[group * TILE:(group + 1) * TILE, :] = part

            @pl.when(core != b)
            def _():
                other_ref[group * TILE:(group + 1) * TILE, :] = part


def combine(core_ref, own_ref, other_ref, scale_ref, out_ref):
    total = (own_ref[...] + other_ref[1 - core_ref[0]]) * scale_ref[...]
    total = total.astype(jnp.bfloat16)
    for k in range(4):
        out_ref[k] = total[k * SUB:(k + 1) * SUB, :]


def dense(part_ref, panel_ref, weight_ref, cot_ref, degree_ref, act_ref, spread_ref, pair_ref):
    scale = degree_scale(degree_ref[pl.ds(part_ref[0], 1), :])
    rows = jnp.concatenate([panel_ref[p] for p in range(4)], axis=1)
    pre_act = jnp.dot(rows, weight_ref[...], preferred_element_type=jnp.float32)
    output, slope = gelu_parts(pre_act)
    act_ref[...] = output.astype(jnp.bfloat16)
    pre_grad = (cot_ref[...].astype(jnp.float32) * slope).astype(jnp.bfloat16)
    pair_ref[0:SUB, :] = rows
    pair_ref[SUB:TILE, :] = pre_grad
    spread = (nt(pre_grad, weight_ref[...]) * scale).astype(jnp.bfloat16)
    for p in range(4):
        spread_ref[p] = spread[:, p * TILE:(p + 1) * TILE]


def weight_terms(core_ref, pair_ref, out_ref):
    half = pl.ds(pl.multiple_of(core_ref[0] * 256, 256), 256)
    rows = jnp.concatenate([pair_ref[b, 0:SUB, half] for b in range(2)], axis=0)
    grads = jnp.concatenate([pair_ref[b, SUB:TILE, :] for b in range(2)], axis=0)
    terms = lax.dot_general(rows, grads, (((0,), (0,)), ((), ())), preferred_element_type=jnp.float32)
    out_ref[...] = terms.astype(jnp.bfloat16)


def sum_first(ref, first=0, last=None):
    total = ref[0, first:last].astype(jnp.float32)
    for s in range(1, ref.shape[0]):
        total = total + ref[s, first:last].astype(jnp.float32)
    return total.astype(jnp.bfloat16)


def pack_panels(part_ref, spread_ref, out_ref):
    total = sum_first(part_ref)
    piece = jnp.concatenate([total[:, p * TILE:(p + 1) * TILE] for p in range(4)], axis=0)
    for p in range(4):
        out_ref[p, 0:SUB, :] = spread_ref[p]
        out_ref[p, SUB:TILE, :] = piece


def merge_panels(panel_ref, out_ref):
    for i in range(4):
        out_ref[i * SUB:(i + 1) * SUB, :] = panel_ref[i, 0:SUB, :]
    out_ref[NB:NB + SUB, :] = sum_first(panel_ref, SUB, TILE)


def spread_back(adj_ref, ring_ref, out_ref, grad):
    for i in range(4):
        grad[i * NB:(i + 1) * NB, :] = ring_ref[i, 0:NB, :]
    piece = sum_first(ring_ref, NB, NB + SUB)
    for i in range(8):
        rows = adj_ref[i * 256:(i + 1) * 256, :]
        terms = jnp.dot(rows, grad[...], preferred_element_type=jnp.float32).astype(jnp.bfloat16)
        for k in range(4):
            out_ref[i * 4 + k, 0:SUB, :] = terms[k * SUB:(k + 1) * SUB, :]
            out_ref[i * 4 + k, SUB:TILE, :] = piece


def finish(plane_ref, scale_ref, feature_ref, weight_ref):
    total = plane_ref[0, 0:SUB, :].astype(jnp.float32)
    for s in range(1, 32):
        total = total + plane_ref[s, 0:SUB, :].astype(jnp.float32)
    feature_ref[...] = (total * scale_ref[...]).astype(jnp.bfloat16)
    for s in range(32):
        for p in range(4):
            at = (s % 2) * 256 + (s // 2) * 16
            weight_ref[at:at + 16, p * TILE:(p + 1) * TILE] = plane_ref[
                s, SUB + p * 16:SUB + (p + 1) * 16, :
            ].astype(jnp.float32)


def local(features, weight, cotangent, tile_slot, tile_count, tile_edges, deg_dst, deg_src):
    bf16 = jnp.bfloat16
    shape = jax.ShapeDtypeStruct
    zh, core, zl = lax.axis_index("zh"), lax.axis_index("c"), lax.axis_index("zl")

    piece, src_scale = call(
        prepare,
        (shape((208, TILE), bf16), shape((SUB, 1), jnp.float32)),
        [SMEM, HBM, HBM, HBM, HBM],
        [
            pltpu.VMEM((SUB, TILE), bf16),
            pltpu.VMEM((1, SUB), jnp.int32),
            pltpu.VMEM((1, SLOTS), jnp.int32),
            pltpu.VMEM((SLOTS, 512), jnp.int32),
            pltpu.SemaphoreType.DMA((4,)),
        ],
        micros=1,
        name="prepare",
        limit=62,
    )(tile_count, features, deg_src[None], tile_slot, tile_edges)
    code = call(
        mark_edges,
        shape((SLOTS + 8, 512), jnp.int32),
        [SMEM, VMEM, VMEM],
        micros=1,
        name="mark_edges",
    )(tile_count, tile_slot, tile_edges)
    ring_piece = lax.all_gather(piece, "zh")
    codes = lax.all_gather(code, "c")
    slots = codes[:, SLOTS, :TILE]

    plane_sources = lax.all_to_all(jnp.broadcast_to(ring_piece[:, :SUB], (16, 4, SUB, TILE)), ("x", "y"), 0, 0)
    tiles, dst_scale = call(
        build_forward,
        (shape((2, TILE, SLOTS * SUB), bf16), shape((NB, 1), jnp.float32)),
        [SMEM, SMEM, VMEM, VMEM],
        micros=6,
        name="build_forward",
    )(slots, core[None], codes, deg_dst[None])
    plane_sources, tiles = lax.optimization_barrier((plane_sources, tiles))

    own_sum, other_sum = call(
        aggregate,
        (shape((NB, TILE), jnp.float32), shape((NB, TILE), jnp.float32)),
        [SMEM, SMEM, VMEM, VMEM],
        [pltpu.VMEM((2, SLOTS * SUB, 2 * TILE), bf16)],
        name="aggregate",
    )(slots, core[None], tiles, plane_sources.reshape(64 * SUB, TILE))
    aggregated = call(combine, shape((4, SUB, TILE), bf16), [SMEM, VMEM, VMEM, VMEM], micros=1, name="combine")(
        core[None], own_sum, lax.all_gather(other_sum, "c"), dst_scale
    )

    panels = lax.all_to_all(aggregated, "zl", 0, 0)
    activated, spread, pair = call(
        dense,
        (shape((SUB, 512), bf16), shape((4, SUB, TILE), bf16), shape((TILE, 512), bf16)),
        [SMEM] + [VMEM] * 4,
        name="dense",
    )(zl[None], panels, weight, cotangent, deg_dst.reshape(4, SUB))
    terms = call(weight_terms, shape((256, 512), bf16), [SMEM, VMEM], micros=1, name="weight_terms")(
        core[None], lax.all_gather(pair, "c")
    )

    parts = lax.all_to_all(terms.reshape(16, 16, 512), ("x", "y"), 0, 0)
    adjacent = call(
        build_backward,
        shape((2048, 1024), bf16),
        [SMEM, SMEM, VMEM],
        [pltpu.SMEM((4 * SLOTS + 8,), jnp.int32), pltpu.VMEM((4 * TILE, TILE), jnp.int32)],
        micros=6,
        name="build_backward",
    )(ring_piece[:, 192, :SLOTS].astype(jnp.int32).reshape(4 * SLOTS), zh[None], ring_piece)
    parts, adjacent = lax.optimization_barrier((parts, adjacent))
    panels = call(pack_panels, shape((4, TILE, TILE), bf16), [VMEM] * 2, micros=1, name="pack_panels")(parts, spread)
    panels = lax.all_to_all(panels, "zl", 0, 0)
    merged = call(merge_panels, shape((NB + SUB, TILE), bf16), [VMEM], micros=1, name="merge_panels")(panels)
    ring = lax.all_gather(merged, "zh")
    plane = call(
        spread_back,
        shape((32, TILE, TILE), bf16),
        [VMEM] * 2,
        [pltpu.VMEM((1024, TILE), bf16)],
        name="spread_back",
    )(adjacent, ring)
    plane = lax.all_to_all(plane, PLANE, 0, 0)
    feature_grad, weight_grad = call(
        finish, (shape((SUB, TILE), bf16), shape((512, 512), jnp.float32)), [VMEM] * 2, name="finish"
    )(plane, src_scale)
    return (activated, weight_grad, feature_grad)


def solution(mesh):
    fine = Mesh(mesh.devices.reshape([size for _, size in FINE]), [name for name, _ in FINE])
    in_specs = (
        P(ROWS, "zl"),
        P(),
        P(ROWS + ("zl",), None),
        P(ROWS, None),
        P(ROWS),
        P(ROWS, None, None),
        P(ROWS),
        P(ROWS),
    )
    out_specs = (P(ROWS + ("zl",), None), P(), P(ROWS, "zl"))
    return jax.shard_map(local, mesh=fine, in_specs=in_specs, out_specs=out_specs, check_vma=False)
```

```python
import jax
import jax.numpy as jnp
from jax import lax
from jax.experimental import pallas as pl
from jax.experimental.pallas import tpu as pltpu
from jax.sharding import Mesh, PartitionSpec as P

TILE = 128
NB = 256
SUB = 64
SLOTS = 32
SQRT_TWO_PI = 0.7978845608028654
CUBIC = 0.044715
ROWS = ("zh", "x", "y", "c")
PLANE = ("x", "y", "c")
FINE = (("zh", 4), ("x", 4), ("y", 4), ("c", 2), ("zl", 4))

VMEM = pl.BlockSpec(memory_space=pltpu.VMEM)
SMEM = pl.BlockSpec(memory_space=pltpu.SMEM)
HBM = pl.BlockSpec(memory_space=pltpu.HBM)


def call(kernel, out_shape, in_specs, scratch=(), micros=2, name=None, out_spec=VMEM, limit=24):
    single = not isinstance(out_shape, (tuple, list))
    return pl.pallas_call(
        kernel,
        out_shape=out_shape,
        in_specs=in_specs,
        out_specs=out_spec if single else [out_spec] * len(out_shape),
        scratch_shapes=list(scratch),
        compiler_params=pltpu.CompilerParams(vmem_limit_bytes=limit * 1024 * 1024),
        cost_estimate=pl.CostEstimate(
            flops=int(micros * 1e9), bytes_accessed=int(micros * 1e6), transcendentals=0
        ),
        name=name,
    )


def gelu_parts(values):
    inner = SQRT_TWO_PI * (values + CUBIC * values * values * values)
    tanh_val = jnp.tanh(inner)
    output = 0.5 * values * (1.0 + tanh_val)
    slope = 0.5 * (1.0 + tanh_val) + 0.5 * values * (1.0 - tanh_val * tanh_val) * SQRT_TWO_PI * (
        1.0 + 3.0 * CUBIC * values * values
    )
    return (output, slope)


def column(row):
    n = row.shape[1]
    first = lax.broadcasted_iota(jnp.int32, (n, n), 0)
    second = lax.broadcasted_iota(jnp.int32, (n, n), 1)
    return jnp.sum(jnp.where(first == second, row, 0.0), axis=1, keepdims=True)


def degree_scale(degrees):
    return column(lax.rsqrt(1.0 + degrees.astype(jnp.float32)))


def encode(edges):
    row = edges >> 7
    value = 1.0 + (edges & (TILE - 1)).astype(jnp.float32) * (1.0 / TILE)
    value = value * jnp.float32(2.0**-32)
    for bit in range(6):
        value = value * jnp.where(((row >> bit) & 1) == 1, jnp.float32(2.0 ** (1 << bit)), jnp.float32(1.0))
    return jnp.where(row >= SUB, -value, value)


def decode(values):
    values = values.astype(jnp.float32)
    rest = jnp.abs(values) * jnp.float32(2.0**32)
    row = jnp.where(values < 0.0, SUB, 0)
    for bit in range(5, -1, -1):
        big = rest >= jnp.float32(2.0 ** (1 << bit))
        rest = jnp.where(big, rest * jnp.float32(2.0 ** -(1 << bit)), rest)
        row = row + jnp.where(big, 1 << bit, 0)
    col = ((rest - 1.0) * TILE).astype(jnp.int32)
    return jnp.where(values == 0.0, -1, row * TILE + col)


def onehot(index, rows=TILE):
    positions = lax.broadcasted_iota(jnp.int32, (rows, index.shape[1]), 0)
    return jnp.where(positions == index, jnp.float32(1.0), jnp.float32(0.0)).astype(jnp.bfloat16)


def nt(left, right):
    return lax.dot_general(left, right, (((1,), (1,)), ((), ())), preferred_element_type=jnp.float32)


def start_copies(sems, *pairs):
    copies = [pltpu.make_async_copy(source, target, sems.at[i]) for i, (source, target) in enumerate(pairs)]
    for copy in copies:
        copy.start()
    return copies


def slot_row(count, slots):
    place = lax.broadcasted_iota(jnp.int32, (1, SLOTS), 1)
    rest = jnp.where(lax.broadcasted_iota(jnp.int32, (1, TILE - SLOTS), 1) == 0, count, 0)
    return jnp.concatenate([jnp.where(place < count, slots & 127, -1), rest], axis=1)


def prepare(count_ref, feature_hbm, degree_hbm, slot_hbm, edge_hbm, out_ref, scale_ref, feature, degree, slot, edge, sems):
    copies = start_copies(
        sems, (degree_hbm, degree), (feature_hbm, feature), (slot_hbm, slot), (edge_hbm.at[0], edge)
    )
    count = count_ref[0]
    copies[0].wait()
    scale = degree_scale(degree[...])
    scale_ref[...] = scale
    copies[1].wait()
    scaled = (feature[...].astype(jnp.float32) * scale).astype(jnp.bfloat16)
    copies[2].wait()
    slots = slot_row(count, slot[...])
    slots = jnp.broadcast_to(slots.astype(jnp.float32), (16, TILE)).astype(jnp.bfloat16)
    copies[3].wait()
    live = lax.broadcasted_iota(jnp.int32, edge.shape, 0) < count
    codes = jnp.where(live, encode(edge[...]), 0.0).astype(jnp.bfloat16)
    out_ref[0:SUB, :] = scaled
    for p in range(4):
        out_ref[SUB + p * SLOTS:SUB + (p + 1) * SLOTS, :] = codes[:, p * TILE:(p + 1) * TILE]
    out_ref[192:208, :] = slots


def mark_edges(count_ref, slot_ref, edge_ref, code_ref):
    count = count_ref[0]
    row = jnp.broadcast_to(slot_row(count, slot_ref[...]), (8, TILE))
    code_ref[SLOTS:SLOTS + 8, :] = jnp.concatenate([row] * 4, axis=1)
    edges = edge_ref[0]
    live = lax.broadcasted_iota(jnp.int32, edges.shape, 0) < count
    code_ref[0:SLOTS, :] = jnp.where(live, edges, -1)


def build_forward(slot_ref, core_ref, code_ref, degree_ref, tiles_ref, scale_ref):
    scale_ref[...] = degree_scale(degree_ref[...])
    tiles_ref[...] = jnp.zeros_like(tiles_ref)
    first = core_ref[0] * SUB
    for b in range(2):

        def step(group, carry):
            for k in range(2):
                pair = []
                for parity in range(2):
                    code = code_ref[b, pl.ds(group * 4 + k * 2 + parity, 1), :]
                    row = onehot(code >> 7)
                    pair.append(nt(row, onehot((code & (TILE - 1)) - first, SUB)))
                lane = pl.multiple_of((group * 2 + k) * TILE, TILE)
                tiles_ref[b, :, pl.ds(lane, TILE)] = jnp.concatenate(pair, axis=1).astype(jnp.bfloat16)
            return carry

        lax.fori_loop(0, (slot_ref[b, SLOTS] + 3) >> 2, step, 0)


def build_backward(slot_ref, quarter_ref, ring_ref, out_ref, list_ref, code_ref):
    out_ref[...] = jnp.zeros_like(out_ref)
    for i in range(4):
        code_ref[i * TILE:(i + 1) * TILE, :] = decode(ring_ref[i, SUB:192, :])
    quarter = quarter_ref[0]
    total = slot_ref.shape[0]

    def scan(i, n):
        slot = slot_ref[i]
        hit = jnp.logical_and(slot >= 0, ((slot & 63) >> 4) == quarter)

        @pl.when(hit)
        def _():
            for k in range(4):
                list_ref[n + k] = i

        return n + hit.astype(jnp.int32)

    found = lax.fori_loop(0, total, scan, 0)

    def step(group, carry):
        for k in range(4):
            i = list_ref[group * 4 + k]
            slot = slot_ref[i]
            block = i >> 5
            at = block * TILE + (i & 31)
            code = jnp.concatenate([code_ref[pl.ds(at + p * SLOTS, 1), :] for p in range(4)], axis=1)
            tile = nt(onehot(code & (TILE - 1)), onehot(code >> 7)).astype(jnp.bfloat16)
            at = pl.multiple_of((slot & 15) * TILE, TILE)
            lane = pl.multiple_of((block * 2 + (slot >> 6)) * TILE, TILE)
            out_ref[pl.ds(at, TILE), pl.ds(lane, TILE)] = tile
        return carry

    lax.fori_loop(0, (found + 3) >> 2, step, 0)


def aggregate(slot_ref, core_ref, tiles_ref, source_ref, own_ref, other_ref, picked):
    core = core_ref[0]
    for b in range(2):
        picked[b] = jnp.zeros((SLOTS * SUB, 2 * TILE), jnp.bfloat16)
        for j in range(SLOTS):
            slot = slot_ref[b, j]
            tile = slot & 63
            at = pl.multiple_of(((tile & 15) * 4 + (tile >> 4)) * SUB, SUB)
            lane = pl.multiple_of(((slot >> 6) & 1) * TILE, TILE)
            picked[b, j * SUB:(j + 1) * SUB, pl.ds(lane, TILE)] = source_ref[pl.ds(at, SUB), :]
        total = jnp.dot(tiles_ref[b], picked[b], preferred_element_type=jnp.float32)
        for group in range(2):
            part = total[:, group * TILE:(group + 1) * TILE]

            @pl.when(core == b)
            def _():
                own_ref[group * TILE:(group + 1) * TILE, :] = part

            @pl.when(core != b)
            def _():
                other_ref[group * TILE:(group + 1) * TILE, :] = part


def combine(core_ref, own_ref, other_ref, scale_ref, out_ref):
    total = (own_ref[...] + other_ref[1 - core_ref[0]]) * scale_ref[...]
    total = total.astype(jnp.bfloat16)
    for k in range(4):
        out_ref[k] = total[k * SUB:(k + 1) * SUB, :]


def dense(part_ref, panel_ref, weight_ref, cot_ref, degree_ref, act_ref, spread_ref, term_ref):
    scale = degree_scale(degree_ref[pl.ds(part_ref[0], 1), :])
    rows = jnp.concatenate([panel_ref[p] for p in range(4)], axis=1)
    pre_act = jnp.dot(rows, weight_ref[...], preferred_element_type=jnp.float32)
    output, slope = gelu_parts(pre_act)
    act_ref[...] = output.astype(jnp.bfloat16)
    pre_grad = (cot_ref[...].astype(jnp.float32) * slope).astype(jnp.bfloat16)
    spread = (nt(pre_grad, weight_ref[...]) * scale).astype(jnp.bfloat16)
    for p in range(4):
        spread_ref[p] = spread[:, p * TILE:(p + 1) * TILE]
    terms = lax.dot_general(rows, pre_grad, (((0,), (0,)), ((), ())), preferred_element_type=jnp.float32)
    term_ref[...] = terms.astype(jnp.bfloat16)


def sum_first(ref, first=0, last=None):
    total = ref[0, first:last].astype(jnp.float32)
    for s in range(1, ref.shape[0]):
        total = total + ref[s, first:last].astype(jnp.float32)
    return total.astype(jnp.bfloat16)


def pack_panels(part_ref, spread_ref, out_ref):
    total = sum_first(part_ref)
    piece = jnp.concatenate([total[:, p * TILE:(p + 1) * TILE] for p in range(4)], axis=0)
    for p in range(4):
        out_ref[p, 0:SUB, :] = spread_ref[p]
        out_ref[p, SUB:TILE, :] = piece


def merge_panels(panel_ref, out_ref):
    for i in range(4):
        out_ref[i * SUB:(i + 1) * SUB, :] = panel_ref[i, 0:SUB, :]
    out_ref[NB:NB + SUB, :] = sum_first(panel_ref, SUB, TILE)


def spread_back(adj_ref, ring_ref, out_ref, grad):
    for i in range(4):
        grad[i * NB:(i + 1) * NB, :] = ring_ref[i, 0:NB, :]
    piece = sum_first(ring_ref, NB, NB + SUB)
    for i in range(8):
        rows = adj_ref[i * 256:(i + 1) * 256, :]
        terms = jnp.dot(rows, grad[...], preferred_element_type=jnp.float32).astype(jnp.bfloat16)
        for k in range(4):
            out_ref[i * 4 + k, 0:SUB, :] = terms[k * SUB:(k + 1) * SUB, :]
            out_ref[i * 4 + k, SUB:TILE, :] = piece


def finish(plane_ref, scale_ref, feature_ref, weight_ref):
    total = plane_ref[0, 0:SUB, :].astype(jnp.float32)
    for s in range(1, 32):
        total = total + plane_ref[s, 0:SUB, :].astype(jnp.float32)
    feature_ref[...] = (total * scale_ref[...]).astype(jnp.bfloat16)
    for s in range(32):
        for p in range(4):
            weight_ref[s * 16:(s + 1) * 16, p * TILE:(p + 1) * TILE] = plane_ref[
                s, SUB + p * 16:SUB + (p + 1) * 16, :
            ].astype(jnp.float32)


def local(features, weight, cotangent, tile_slot, tile_count, tile_edges, deg_dst, deg_src):
    bf16 = jnp.bfloat16
    shape = jax.ShapeDtypeStruct
    zh, core, zl = lax.axis_index("zh"), lax.axis_index("c"), lax.axis_index("zl")

    piece, src_scale = call(
        prepare,
        (shape((208, TILE), bf16), shape((SUB, 1), jnp.float32)),
        [SMEM, HBM, HBM, HBM, HBM],
        [
            pltpu.VMEM((SUB, TILE), bf16),
            pltpu.VMEM((1, SUB), jnp.int32),
            pltpu.VMEM((1, SLOTS), jnp.int32),
            pltpu.VMEM((SLOTS, 512), jnp.int32),
            pltpu.SemaphoreType.DMA((4,)),
        ],
        micros=1,
        name="prepare",
        limit=62,
    )(tile_count, features, deg_src[None], tile_slot, tile_edges)
    code = call(
        mark_edges,
        shape((SLOTS + 8, 512), jnp.int32),
        [SMEM, VMEM, VMEM],
        micros=1,
        name="mark_edges",
    )(tile_count, tile_slot, tile_edges)
    ring_piece = lax.all_gather(piece, "zh")
    codes = lax.all_gather(code, "c")
    slots = codes[:, SLOTS, :TILE]

    plane_sources = lax.all_to_all(jnp.broadcast_to(ring_piece[:, :SUB], (16, 4, SUB, TILE)), ("x", "y"), 0, 0)
    tiles, dst_scale = call(
        build_forward,
        (shape((2, TILE, SLOTS * SUB), bf16), shape((NB, 1), jnp.float32)),
        [SMEM, SMEM, VMEM, VMEM],
        micros=6,
        name="build_forward",
    )(slots, core[None], codes, deg_dst[None])
    plane_sources, tiles = lax.optimization_barrier((plane_sources, tiles))

    own_sum, other_sum = call(
        aggregate,
        (shape((NB, TILE), jnp.float32), shape((NB, TILE), jnp.float32)),
        [SMEM, SMEM, VMEM, VMEM],
        [pltpu.VMEM((2, SLOTS * SUB, 2 * TILE), bf16)],
        name="aggregate",
    )(slots, core[None], tiles, plane_sources.reshape(64 * SUB, TILE))
    aggregated = call(combine, shape((4, SUB, TILE), bf16), [SMEM, VMEM, VMEM, VMEM], micros=1, name="combine")(
        core[None], own_sum, lax.all_gather(other_sum, "c"), dst_scale
    )

    panels = lax.all_to_all(aggregated, "zl", 0, 0)
    activated, spread, terms = call(
        dense,
        (shape((SUB, 512), bf16), shape((4, SUB, TILE), bf16), shape((512, 512), bf16)),
        [SMEM] + [VMEM] * 4,
        name="dense",
    )(zl[None], panels, weight, cotangent, deg_dst.reshape(4, SUB))

    parts = lax.all_to_all(terms.reshape(32, 16, 512), PLANE, 0, 0)
    adjacent = call(
        build_backward,
        shape((2048, 1024), bf16),
        [SMEM, SMEM, VMEM],
        [pltpu.SMEM((4 * SLOTS + 8,), jnp.int32), pltpu.VMEM((4 * TILE, TILE), jnp.int32)],
        micros=6,
        name="build_backward",
    )(ring_piece[:, 192, :SLOTS].astype(jnp.int32).reshape(4 * SLOTS), zh[None], ring_piece)
    parts, adjacent = lax.optimization_barrier((parts, adjacent))
    panels = call(pack_panels, shape((4, TILE, TILE), bf16), [VMEM] * 2, micros=1, name="pack_panels")(parts, spread)
    panels = lax.all_to_all(panels, "zl", 0, 0)
    merged = call(merge_panels, shape((NB + SUB, TILE), bf16), [VMEM], micros=1, name="merge_panels")(panels)
    ring = lax.all_gather(merged, "zh")
    plane = call(
        spread_back,
        shape((32, TILE, TILE), bf16),
        [VMEM] * 2,
        [pltpu.VMEM((1024, TILE), bf16)],
        name="spread_back",
    )(adjacent, ring)
    plane = lax.all_to_all(plane, PLANE, 0, 0)
    feature_grad, weight_grad = call(
        finish, (shape((SUB, TILE), bf16), shape((512, 512), jnp.float32)), [VMEM] * 2, name="finish"
    )(plane, src_scale)
    return (activated, weight_grad, feature_grad)


def solution(mesh):
    fine = Mesh(mesh.devices.reshape([size for _, size in FINE]), [name for name, _ in FINE])
    in_specs = (
        P(ROWS, "zl"),
        P(),
        P(ROWS + ("zl",), None),
        P(ROWS, None),
        P(ROWS),
        P(ROWS, None, None),
        P(ROWS),
        P(ROWS),
    )
    out_specs = (P(ROWS + ("zl",), None), P(), P(ROWS, "zl"))
    return jax.shard_map(local, mesh=fine, in_specs=in_specs, out_specs=out_specs, check_vma=False)
```

```python
import jax
import jax.numpy as jnp
from jax import lax
from jax.experimental import pallas as pl
from jax.experimental.pallas import tpu as pltpu
from jax.sharding import Mesh, PartitionSpec as P

TILE = 128
NB = 256
SUB = 64
SLOTS = 32
SQRT_TWO_PI = 0.7978845608028654
CUBIC = 0.044715
ROWS = ("zh", "x", "y", "c")
PLANE = ("x", "y", "c")
FINE = (("zh", 4), ("x", 4), ("y", 4), ("c", 2), ("zl", 4))

VMEM = pl.BlockSpec(memory_space=pltpu.VMEM)
SMEM = pl.BlockSpec(memory_space=pltpu.SMEM)
HBM = pl.BlockSpec(memory_space=pltpu.HBM)


def call(kernel, out_shape, in_specs, scratch=(), micros=2, name=None, out_spec=VMEM, limit=24):
    single = not isinstance(out_shape, (tuple, list))
    return pl.pallas_call(
        kernel,
        out_shape=out_shape,
        in_specs=in_specs,
        out_specs=out_spec if single else [out_spec] * len(out_shape),
        scratch_shapes=list(scratch),
        compiler_params=pltpu.CompilerParams(vmem_limit_bytes=limit * 1024 * 1024),
        cost_estimate=pl.CostEstimate(
            flops=int(micros * 1e9), bytes_accessed=int(micros * 1e6), transcendentals=0
        ),
        name=name,
    )


def gelu_parts(values):
    inner = SQRT_TWO_PI * (values + CUBIC * values * values * values)
    tanh_val = jnp.tanh(inner)
    output = 0.5 * values * (1.0 + tanh_val)
    slope = 0.5 * (1.0 + tanh_val) + 0.5 * values * (1.0 - tanh_val * tanh_val) * SQRT_TWO_PI * (
        1.0 + 3.0 * CUBIC * values * values
    )
    return (output, slope)


def column(row):
    n = row.shape[1]
    first = lax.broadcasted_iota(jnp.int32, (n, n), 0)
    second = lax.broadcasted_iota(jnp.int32, (n, n), 1)
    return jnp.sum(jnp.where(first == second, row, 0.0), axis=1, keepdims=True)


def degree_scale(degrees):
    return column(lax.rsqrt(1.0 + degrees.astype(jnp.float32)))


def encode(edges):
    row = edges >> 7
    value = 1.0 + (edges & (TILE - 1)).astype(jnp.float32) * (1.0 / TILE)
    value = value * jnp.float32(2.0**-32)
    for bit in range(6):
        value = value * jnp.where(((row >> bit) & 1) == 1, jnp.float32(2.0 ** (1 << bit)), jnp.float32(1.0))
    return jnp.where(row >= SUB, -value, value)


def decode(values):
    values = values.astype(jnp.float32)
    rest = jnp.abs(values) * jnp.float32(2.0**32)
    row = jnp.where(values < 0.0, SUB, 0)
    for bit in range(5, -1, -1):
        big = rest >= jnp.float32(2.0 ** (1 << bit))
        rest = jnp.where(big, rest * jnp.float32(2.0 ** -(1 << bit)), rest)
        row = row + jnp.where(big, 1 << bit, 0)
    col = ((rest - 1.0) * TILE).astype(jnp.int32)
    return jnp.where(values == 0.0, -1, row * TILE + col)


def onehot(index, rows=TILE):
    positions = lax.broadcasted_iota(jnp.int32, (rows, index.shape[1]), 0)
    return jnp.where(positions == index, jnp.float32(1.0), jnp.float32(0.0)).astype(jnp.bfloat16)


def nt(left, right):
    return lax.dot_general(left, right, (((1,), (1,)), ((), ())), preferred_element_type=jnp.float32)


def start_copies(sems, *pairs):
    copies = [pltpu.make_async_copy(source, target, sems.at[i]) for i, (source, target) in enumerate(pairs)]
    for copy in copies:
        copy.start()
    return copies


def slot_row(count, slots):
    place = lax.broadcasted_iota(jnp.int32, (1, SLOTS), 1)
    rest = jnp.where(lax.broadcasted_iota(jnp.int32, (1, TILE - SLOTS), 1) == 0, count, 0)
    return jnp.concatenate([jnp.where(place < count, slots & 127, -1), rest], axis=1)


def prepare(count_ref, feature_hbm, degree_hbm, slot_hbm, edge_hbm, out_ref, scale_ref, feature, degree, slot, edge, sems):
    copies = start_copies(
        sems, (degree_hbm, degree), (feature_hbm, feature), (slot_hbm, slot), (edge_hbm.at[0], edge)
    )
    count = count_ref[0]
    copies[0].wait()
    scale = degree_scale(degree[...])
    scale_ref[...] = scale
    copies[1].wait()
    scaled = (feature[...].astype(jnp.float32) * scale).astype(jnp.bfloat16)
    copies[2].wait()
    slots = slot_row(count, slot[...])
    slots = jnp.broadcast_to(slots.astype(jnp.float32), (16, TILE)).astype(jnp.bfloat16)
    copies[3].wait()
    live = lax.broadcasted_iota(jnp.int32, edge.shape, 0) < count
    codes = jnp.where(live, encode(edge[...]), 0.0).astype(jnp.bfloat16)
    out_ref[0:SUB, :] = scaled
    for p in range(4):
        out_ref[SUB + p * SLOTS:SUB + (p + 1) * SLOTS, :] = codes[:, p * TILE:(p + 1) * TILE]
    out_ref[192:208, :] = slots


def fan_out(ring_ref, out_hbm, sems):
    copies = start_copies(sems, *((ring_ref.at[:, 0:SUB], out_hbm.at[i]) for i in range(16)))
    for copy in copies:
        copy.wait()


def mark_edges(count_ref, slot_ref, edge_ref, code_ref):
    count = count_ref[0]
    row = jnp.broadcast_to(slot_row(count, slot_ref[...]), (8, TILE))
    code_ref[SLOTS:SLOTS + 8, :] = jnp.concatenate([row] * 4, axis=1)
    edges = edge_ref[0]
    live = lax.broadcasted_iota(jnp.int32, edges.shape, 0) < count
    code_ref[0:SLOTS, :] = jnp.where(live, edges, -1)


def build_forward(slot_ref, core_ref, code_ref, degree_ref, tiles_ref, scale_ref):
    scale_ref[...] = degree_scale(degree_ref[...])
    tiles_ref[...] = jnp.zeros_like(tiles_ref)
    first = core_ref[0] * SUB
    for b in range(2):

        def step(group, carry):
            for k in range(2):
                pair = []
                for parity in range(2):
                    code = code_ref[b, pl.ds(group * 4 + k * 2 + parity, 1), :]
                    row = onehot(code >> 7)
                    pair.append(nt(row, onehot((code & (TILE - 1)) - first, SUB)))
                lane = pl.multiple_of((group * 2 + k) * TILE, TILE)
                tiles_ref[b, :, pl.ds(lane, TILE)] = jnp.concatenate(pair, axis=1).astype(jnp.bfloat16)
            return carry

        lax.fori_loop(0, (slot_ref[b, SLOTS] + 3) >> 2, step, 0)


def build_backward(slot_ref, quarter_ref, ring_ref, out_ref, list_ref, code_ref):
    out_ref[...] = jnp.zeros_like(out_ref)
    for i in range(4):
        code_ref[i * TILE:(i + 1) * TILE, :] = decode(ring_ref[i, SUB:192, :])
    quarter = quarter_ref[0]
    total = slot_ref.shape[0]

    def scan(i, n):
        slot = slot_ref[i]
        hit = jnp.logical_and(slot >= 0, ((slot & 63) >> 4) == quarter)

        @pl.when(hit)
        def _():
            for k in range(4):
                list_ref[n + k] = i

        return n + hit.astype(jnp.int32)

    found = lax.fori_loop(0, total, scan, 0)

    def step(group, carry):
        for k in range(4):
            i = list_ref[group * 4 + k]
            slot = slot_ref[i]
            block = i >> 5
            at = block * TILE + (i & 31)
            code = jnp.concatenate([code_ref[pl.ds(at + p * SLOTS, 1), :] for p in range(4)], axis=1)
            tile = nt(onehot(code & (TILE - 1)), onehot(code >> 7)).astype(jnp.bfloat16)
            at = pl.multiple_of((slot & 15) * TILE, TILE)
            lane = pl.multiple_of((block * 2 + (slot >> 6)) * TILE, TILE)
            out_ref[pl.ds(at, TILE), pl.ds(lane, TILE)] = tile
        return carry

    lax.fori_loop(0, (found + 3) >> 2, step, 0)


def aggregate(slot_ref, core_ref, tiles_ref, source_ref, own_ref, other_ref, picked):
    core = core_ref[0]
    for b in range(2):
        for j in range(SLOTS):
            slot = slot_ref[b, j]
            tile = slot & 63
            at = pl.multiple_of(((tile & 15) * 4 + (tile >> 4)) * SUB, SUB)
            rows = source_ref[pl.ds(at, SUB), :]
            first = ((slot >> 6) & 1) == 0
            picked[b, j * SUB:(j + 1) * SUB, 0:TILE] = jnp.where(first, rows, jnp.zeros_like(rows))
            picked[b, j * SUB:(j + 1) * SUB, TILE:2 * TILE] = jnp.where(first, jnp.zeros_like(rows), rows)
        total = jnp.dot(tiles_ref[b], picked[b], preferred_element_type=jnp.float32)
        for group in range(2):
            part = total[:, group * TILE:(group + 1) * TILE]

            @pl.when(core == b)
            def _():
                own_ref[group * TILE:(group + 1) * TILE, :] = part

            @pl.when(core != b)
            def _():
                other_ref[group * TILE:(group + 1) * TILE, :] = part


def combine(core_ref, own_ref, other_ref, scale_ref, out_ref):
    total = (own_ref[...] + other_ref[1 - core_ref[0]]) * scale_ref[...]
    total = total.astype(jnp.bfloat16)
    for k in range(4):
        out_ref[k] = total[k * SUB:(k + 1) * SUB, :]


def dense(part_ref, panel_ref, weight_ref, cot_ref, degree_ref, act_ref, spread_ref, term_ref):
    scale = degree_scale(degree_ref[pl.ds(part_ref[0], 1), :])
    rows = jnp.concatenate([panel_ref[p] for p in range(4)], axis=1)
    pre_act = jnp.dot(rows, weight_ref[...], preferred_element_type=jnp.float32)
    output, slope = gelu_parts(pre_act)
    act_ref[...] = output.astype(jnp.bfloat16)
    pre_grad = (cot_ref[...].astype(jnp.float32) * slope).astype(jnp.bfloat16)
    spread = (nt(pre_grad, weight_ref[...]) * scale).astype(jnp.bfloat16)
    for p in range(4):
        spread_ref[p] = spread[:, p * TILE:(p + 1) * TILE]
    terms = lax.dot_general(rows, pre_grad, (((0,), (0,)), ((), ())), preferred_element_type=jnp.float32)
    term_ref[...] = terms.astype(jnp.bfloat16)


def sum_first(ref, first=0, last=None):
    total = ref[0, first:last].astype(jnp.float32)
    for s in range(1, ref.shape[0]):
        total = total + ref[s, first:last].astype(jnp.float32)
    return total.astype(jnp.bfloat16)


def pack_panels(part_ref, spread_ref, out_ref):
    total = sum_first(part_ref)
    piece = jnp.concatenate([total[:, p * TILE:(p + 1) * TILE] for p in range(4)], axis=0)
    for p in range(4):
        out_ref[p, 0:SUB, :] = spread_ref[p]
        out_ref[p, SUB:TILE, :] = piece


def merge_panels(panel_ref, out_ref):
    for i in range(4):
        out_ref[i * SUB:(i + 1) * SUB, :] = panel_ref[i, 0:SUB, :]
    out_ref[NB:NB + SUB, :] = sum_first(panel_ref, SUB, TILE)


def spread_back(adj_ref, ring_ref, out_ref, grad):
    for i in range(4):
        grad[i * NB:(i + 1) * NB, :] = ring_ref[i, 0:NB, :]
    piece = sum_first(ring_ref, NB, NB + SUB)
    for i in range(8):
        rows = adj_ref[i * 256:(i + 1) * 256, :]
        terms = jnp.dot(rows, grad[...], preferred_element_type=jnp.float32).astype(jnp.bfloat16)
        for k in range(4):
            out_ref[i * 4 + k, 0:SUB, :] = terms[k * SUB:(k + 1) * SUB, :]
            out_ref[i * 4 + k, SUB:TILE, :] = piece


def finish(plane_ref, scale_ref, feature_ref, weight_ref):
    total = plane_ref[0, 0:SUB, :].astype(jnp.float32)
    for s in range(1, 32):
        total = total + plane_ref[s, 0:SUB, :].astype(jnp.float32)
    feature_ref[...] = (total * scale_ref[...]).astype(jnp.bfloat16)
    for s in range(32):
        for p in range(4):
            weight_ref[s * 16:(s + 1) * 16, p * TILE:(p + 1) * TILE] = plane_ref[
                s, SUB + p * 16:SUB + (p + 1) * 16, :
            ].astype(jnp.float32)


def local(features, weight, cotangent, tile_slot, tile_count, tile_edges, deg_dst, deg_src):
    bf16 = jnp.bfloat16
    shape = jax.ShapeDtypeStruct
    zh, core, zl = lax.axis_index("zh"), lax.axis_index("c"), lax.axis_index("zl")

    piece, src_scale = call(
        prepare,
        (shape((208, TILE), bf16), shape((SUB, 1), jnp.float32)),
        [SMEM, HBM, HBM, HBM, HBM],
        [
            pltpu.VMEM((SUB, TILE), bf16),
            pltpu.VMEM((1, SUB), jnp.int32),
            pltpu.VMEM((1, SLOTS), jnp.int32),
            pltpu.VMEM((SLOTS, 512), jnp.int32),
            pltpu.SemaphoreType.DMA((4,)),
        ],
        micros=1,
        name="prepare",
        limit=62,
    )(tile_count, features, deg_src[None], tile_slot, tile_edges)
    code = call(
        mark_edges,
        shape((SLOTS + 8, 512), jnp.int32),
        [SMEM, VMEM, VMEM],
        micros=1,
        name="mark_edges",
    )(tile_count, tile_slot, tile_edges)
    ring_piece = lax.all_gather(piece, "zh")
    codes = lax.all_gather(code, "c")
    slots = codes[:, SLOTS, :TILE]

    copies = call(
        fan_out,
        shape((16, 4, SUB, TILE), bf16),
        [VMEM],
        [pltpu.SemaphoreType.DMA((16,))],
        micros=1,
        name="fan_out",
        out_spec=HBM,
    )(ring_piece)
    plane_sources = lax.all_to_all(copies, ("x", "y"), 0, 0)
    tiles, dst_scale = call(
        build_forward,
        (shape((2, TILE, SLOTS * SUB), bf16), shape((NB, 1), jnp.float32)),
        [SMEM, SMEM, VMEM, VMEM],
        micros=6,
        name="build_forward",
    )(slots, core[None], codes, deg_dst[None])
    plane_sources, tiles = lax.optimization_barrier((plane_sources, tiles))

    own_sum, other_sum = call(
        aggregate,
        (shape((NB, TILE), jnp.float32), shape((NB, TILE), jnp.float32)),
        [SMEM, SMEM, VMEM, VMEM],
        [pltpu.VMEM((2, SLOTS * SUB, 2 * TILE), bf16)],
        name="aggregate",
    )(slots, core[None], tiles, plane_sources.reshape(64 * SUB, TILE))
    aggregated = call(combine, shape((4, SUB, TILE), bf16), [SMEM, VMEM, VMEM, VMEM], micros=1, name="combine")(
        core[None], own_sum, lax.all_gather(other_sum, "c"), dst_scale
    )

    panels = lax.all_to_all(aggregated, "zl", 0, 0)
    activated, spread, terms = call(
        dense,
        (shape((SUB, 512), bf16), shape((4, SUB, TILE), bf16), shape((512, 512), bf16)),
        [SMEM] + [VMEM] * 4,
        name="dense",
    )(zl[None], panels, weight, cotangent, deg_dst.reshape(4, SUB))

    parts = lax.all_to_all(terms.reshape(32, 16, 512), PLANE, 0, 0)
    adjacent = call(
        build_backward,
        shape((2048, 1024), bf16),
        [SMEM, SMEM, VMEM],
        [pltpu.SMEM((4 * SLOTS + 8,), jnp.int32), pltpu.VMEM((4 * TILE, TILE), jnp.int32)],
        micros=6,
        name="build_backward",
    )(ring_piece[:, 192, :SLOTS].astype(jnp.int32).reshape(4 * SLOTS), zh[None], ring_piece)
    parts, adjacent = lax.optimization_barrier((parts, adjacent))
    panels = call(pack_panels, shape((4, TILE, TILE), bf16), [VMEM] * 2, micros=1, name="pack_panels")(parts, spread)
    panels = lax.all_to_all(panels, "zl", 0, 0)
    merged = call(merge_panels, shape((NB + SUB, TILE), bf16), [VMEM], micros=1, name="merge_panels")(panels)
    ring = lax.all_gather(merged, "zh")
    plane = call(
        spread_back,
        shape((32, TILE, TILE), bf16),
        [VMEM] * 2,
        [pltpu.VMEM((1024, TILE), bf16)],
        name="spread_back",
    )(adjacent, ring)
    plane = lax.all_to_all(plane, PLANE, 0, 0)
    feature_grad, weight_grad = call(
        finish, (shape((SUB, TILE), bf16), shape((512, 512), jnp.float32)), [VMEM] * 2, name="finish"
    )(plane, src_scale)
    return (activated, weight_grad, feature_grad)


def solution(mesh):
    fine = Mesh(mesh.devices.reshape([size for _, size in FINE]), [name for name, _ in FINE])
    in_specs = (
        P(ROWS, "zl"),
        P(),
        P(ROWS + ("zl",), None),
        P(ROWS, None),
        P(ROWS),
        P(ROWS, None, None),
        P(ROWS),
        P(ROWS),
    )
    out_specs = (P(ROWS + ("zl",), None), P(), P(ROWS, "zl"))
    return jax.shard_map(local, mesh=fine, in_specs=in_specs, out_specs=out_specs, check_vma=False)
```

```python
import jax
import jax.numpy as jnp
from jax import lax
from jax.experimental import pallas as pl
from jax.experimental.pallas import tpu as pltpu
from jax.sharding import Mesh, PartitionSpec as P

TILE = 128
NB = 256
SUB = 64
SLOTS = 32
SQRT_TWO_PI = 0.7978845608028654
CUBIC = 0.044715
ROWS = ("zh", "x", "y", "c")
PLANE = ("x", "y", "c")
FINE = (("zh", 4), ("x", 4), ("y", 4), ("c", 2), ("zl", 4))

VMEM = pl.BlockSpec(memory_space=pltpu.VMEM)
SMEM = pl.BlockSpec(memory_space=pltpu.SMEM)
HBM = pl.BlockSpec(memory_space=pltpu.HBM)


def call(kernel, out_shape, in_specs, scratch=(), micros=2, name=None, out_spec=VMEM, limit=24):
    single = not isinstance(out_shape, (tuple, list))
    return pl.pallas_call(
        kernel,
        out_shape=out_shape,
        in_specs=in_specs,
        out_specs=out_spec if single else [out_spec] * len(out_shape),
        scratch_shapes=list(scratch),
        compiler_params=pltpu.CompilerParams(vmem_limit_bytes=limit * 1024 * 1024),
        cost_estimate=pl.CostEstimate(
            flops=int(micros * 1e9), bytes_accessed=int(micros * 1e6), transcendentals=0
        ),
        name=name,
    )


def gelu_parts(values):
    inner = SQRT_TWO_PI * (values + CUBIC * values * values * values)
    tanh_val = jnp.tanh(inner)
    output = 0.5 * values * (1.0 + tanh_val)
    slope = 0.5 * (1.0 + tanh_val) + 0.5 * values * (1.0 - tanh_val * tanh_val) * SQRT_TWO_PI * (
        1.0 + 3.0 * CUBIC * values * values
    )
    return (output, slope)


def column(row):
    n = row.shape[1]
    first = lax.broadcasted_iota(jnp.int32, (n, n), 0)
    second = lax.broadcasted_iota(jnp.int32, (n, n), 1)
    return jnp.sum(jnp.where(first == second, row, 0.0), axis=1, keepdims=True)


def degree_scale(degrees):
    return column(lax.rsqrt(1.0 + degrees.astype(jnp.float32)))


def encode(edges):
    row = edges >> 7
    value = 1.0 + (edges & (TILE - 1)).astype(jnp.float32) * (1.0 / TILE)
    value = value * jnp.float32(2.0**-32)
    for bit in range(6):
        value = value * jnp.where(((row >> bit) & 1) == 1, jnp.float32(2.0 ** (1 << bit)), jnp.float32(1.0))
    return jnp.where(row >= SUB, -value, value)


def decode(values):
    values = values.astype(jnp.float32)
    rest = jnp.abs(values) * jnp.float32(2.0**32)
    row = jnp.where(values < 0.0, SUB, 0)
    for bit in range(5, -1, -1):
        big = rest >= jnp.float32(2.0 ** (1 << bit))
        rest = jnp.where(big, rest * jnp.float32(2.0 ** -(1 << bit)), rest)
        row = row + jnp.where(big, 1 << bit, 0)
    col = ((rest - 1.0) * TILE).astype(jnp.int32)
    return jnp.where(values == 0.0, -1, row * TILE + col)


def onehot(index, rows=TILE):
    positions = lax.broadcasted_iota(jnp.int32, (rows, index.shape[1]), 0)
    return jnp.where(positions == index, jnp.float32(1.0), jnp.float32(0.0)).astype(jnp.bfloat16)


def nt(left, right):
    return lax.dot_general(left, right, (((1,), (1,)), ((), ())), preferred_element_type=jnp.float32)


def start_copies(sems, *pairs):
    copies = [pltpu.make_async_copy(source, target, sems.at[i]) for i, (source, target) in enumerate(pairs)]
    for copy in copies:
        copy.start()
    return copies


def slot_row(count, slots):
    place = lax.broadcasted_iota(jnp.int32, (1, SLOTS), 1)
    rest = jnp.where(lax.broadcasted_iota(jnp.int32, (1, TILE - SLOTS), 1) == 0, count, 0)
    return jnp.concatenate([jnp.where(place < count, slots & 127, -1), rest], axis=1)


def prepare(count_ref, feature_hbm, degree_hbm, slot_hbm, edge_hbm, out_ref, scale_ref, feature, degree, slot, edge, sems):
    copies = start_copies(
        sems, (degree_hbm, degree), (feature_hbm, feature), (slot_hbm, slot), (edge_hbm.at[0], edge)
    )
    count = count_ref[0]
    copies[0].wait()
    scale = degree_scale(degree[...])
    scale_ref[...] = scale
    copies[1].wait()
    scaled = (feature[...].astype(jnp.float32) * scale).astype(jnp.bfloat16)
    copies[2].wait()
    slots = slot_row(count, slot[...])
    slots = jnp.broadcast_to(slots.astype(jnp.float32), (16, TILE)).astype(jnp.bfloat16)
    copies[3].wait()
    live = lax.broadcasted_iota(jnp.int32, edge.shape, 0) < count
    codes = jnp.where(live, encode(edge[...]), 0.0).astype(jnp.bfloat16)
    out_ref[0:SUB, :] = scaled
    for p in range(4):
        out_ref[SUB + p * SLOTS:SUB + (p + 1) * SLOTS, :] = codes[:, p * TILE:(p + 1) * TILE]
    out_ref[192:208, :] = slots


def fan_out(ring_ref, out_hbm, sems):
    copies = start_copies(sems, *((ring_ref.at[:, 0:SUB], out_hbm.at[i]) for i in range(16)))
    for copy in copies:
        copy.wait()


def mark_edges(count_ref, slot_ref, edge_ref, code_ref):
    count = count_ref[0]
    row = jnp.broadcast_to(slot_row(count, slot_ref[...]), (8, TILE))
    code_ref[SLOTS:SLOTS + 8, :] = jnp.concatenate([row] * 4, axis=1)
    edges = edge_ref[0]
    live = lax.broadcasted_iota(jnp.int32, edges.shape, 0) < count
    code_ref[0:SLOTS, :] = jnp.where(live, edges, -1)


def build_forward(slot_ref, core_ref, code_ref, degree_ref, tiles_ref, scale_ref):
    scale_ref[...] = degree_scale(degree_ref[...])
    tiles_ref[...] = jnp.zeros_like(tiles_ref)
    first = core_ref[0] * SUB
    for b in range(2):

        def step(group, carry):
            for k in range(2):
                pair = []
                for parity in range(2):
                    code = code_ref[b, pl.ds(group * 4 + k * 2 + parity, 1), :]
                    row = onehot(code >> 7)
                    pair.append(nt(row, onehot((code & (TILE - 1)) - first, SUB)))
                lane = pl.multiple_of((group * 2 + k) * TILE, TILE)
                tiles_ref[b, :, pl.ds(lane, TILE)] = jnp.concatenate(pair, axis=1).astype(jnp.bfloat16)
            return carry

        lax.fori_loop(0, (slot_ref[b, SLOTS] + 3) >> 2, step, 0)


def build_backward(slot_ref, quarter_ref, ring_ref, out_ref, list_ref, code_ref):
    out_ref[...] = jnp.zeros_like(out_ref)
    for i in range(4):
        code_ref[i * TILE:(i + 1) * TILE, :] = decode(ring_ref[i, SUB:192, :])
    quarter = quarter_ref[0]
    total = slot_ref.shape[0]

    def scan(i, n):
        slot = slot_ref[i]
        hit = jnp.logical_and(slot >= 0, ((slot & 63) >> 4) == quarter)

        @pl.when(hit)
        def _():
            for k in range(4):
                list_ref[n + k] = i

        return n + hit.astype(jnp.int32)

    found = lax.fori_loop(0, total, scan, 0)

    def step(group, carry):
        for k in range(4):
            i = list_ref[group * 4 + k]
            slot = slot_ref[i]
            block = i >> 5
            at = block * TILE + (i & 31)
            code = jnp.concatenate([code_ref[pl.ds(at + p * SLOTS, 1), :] for p in range(4)], axis=1)
            tile = nt(onehot(code & (TILE - 1)), onehot(code >> 7)).astype(jnp.bfloat16)
            at = pl.multiple_of((slot & 15) * TILE, TILE)
            lane = pl.multiple_of((block * 2 + (slot >> 6)) * TILE, TILE)
            out_ref[pl.ds(at, TILE), pl.ds(lane, TILE)] = tile
        return carry

    lax.fori_loop(0, (found + 3) >> 2, step, 0)


def aggregate(slot_ref, core_ref, tiles_ref, source_ref, own_ref, other_ref, picked):
    core = core_ref[0]
    for b in range(2):
        for j in range(SLOTS):
            slot = slot_ref[b, j]
            tile = slot & 63
            at = pl.multiple_of(((tile & 15) * 4 + (tile >> 4)) * SUB, SUB)
            rows = source_ref[pl.ds(at, SUB), :]
            first = ((slot >> 6) & 1) == 0
            picked[b, j * SUB:(j + 1) * SUB, 0:TILE] = jnp.where(first, rows, jnp.zeros_like(rows))
            picked[b, j * SUB:(j + 1) * SUB, TILE:2 * TILE] = jnp.where(first, jnp.zeros_like(rows), rows)
        total = jnp.dot(tiles_ref[b], picked[b], preferred_element_type=jnp.float32)
        for group in range(2):
            part = total[:, group * TILE:(group + 1) * TILE]

            @pl.when(core == b)
            def _():
                own_ref[group * TILE:(group + 1) * TILE, :] = part

            @pl.when(core != b)
            def _():
                other_ref[group * TILE:(group + 1) * TILE, :] = part


def combine(core_ref, own_ref, other_ref, scale_ref, out_ref):
    total = (own_ref[...] + other_ref[1 - core_ref[0]]) * scale_ref[...]
    total = total.astype(jnp.bfloat16)
    for k in range(4):
        out_ref[k] = total[k * SUB:(k + 1) * SUB, :]


def dense(part_ref, panel_ref, weight_ref, cot_ref, degree_ref, act_ref, spread_ref, term_ref):
    scale = degree_scale(degree_ref[pl.ds(part_ref[0], 1), :])
    rows = jnp.concatenate([panel_ref[p] for p in range(4)], axis=1)
    pre_act = jnp.dot(rows, weight_ref[...], preferred_element_type=jnp.float32)
    output, slope = gelu_parts(pre_act)
    act_ref[...] = output.astype(jnp.bfloat16)
    pre_grad = (cot_ref[...].astype(jnp.float32) * slope).astype(jnp.bfloat16)
    spread = (nt(pre_grad, weight_ref[...]) * scale).astype(jnp.bfloat16)
    for p in range(4):
        spread_ref[p] = spread[:, p * TILE:(p + 1) * TILE]
    terms = lax.dot_general(rows, pre_grad, (((0,), (0,)), ((), ())), preferred_element_type=jnp.float32)
    term_ref[...] = terms.astype(jnp.bfloat16)


def sum_first(ref, first=0, last=None):
    total = ref[0, first:last].astype(jnp.float32)
    for s in range(1, ref.shape[0]):
        total = total + ref[s, first:last].astype(jnp.float32)
    return total.astype(jnp.bfloat16)


def pack_panels(part_ref, spread_ref, out_ref):
    total = sum_first(part_ref)
    piece = jnp.concatenate([total[:, p * TILE:(p + 1) * TILE] for p in range(4)], axis=0)
    for p in range(4):
        out_ref[p, 0:SUB, :] = spread_ref[p]
        out_ref[p, SUB:TILE, :] = piece


def merge_panels(panel_ref, out_ref):
    for i in range(4):
        out_ref[i * SUB:(i + 1) * SUB, :] = panel_ref[i, 0:SUB, :]
    out_ref[NB:NB + SUB, :] = sum_first(panel_ref, SUB, TILE)


def spread_back(adj_ref, ring_ref, out_ref, grad):
    for i in range(4):
        grad[i * NB:(i + 1) * NB, :] = ring_ref[i, 0:NB, :]
    piece = sum_first(ring_ref, NB, NB + SUB)
    for i in range(8):
        rows = adj_ref[i * 256:(i + 1) * 256, :]
        terms = jnp.dot(rows, grad[...], preferred_element_type=jnp.float32).astype(jnp.bfloat16)
        for k in range(4):
            out_ref[i * 4 + k, 0:SUB, :] = terms[k * SUB:(k + 1) * SUB, :]
            half = (k % 2) * 32
            out_ref[i * 4 + k, SUB:96, :] = piece[half:half + 32, :]


def finish(plane_ref, scale_ref, feature_ref, weight_ref):
    total = plane_ref[0, 0:SUB, :].astype(jnp.float32)
    for s in range(1, 32):
        total = total + plane_ref[s, 0:SUB, :].astype(jnp.float32)
    feature_ref[...] = (total * scale_ref[...]).astype(jnp.bfloat16)
    for s in range(32):
        for p in range(2):
            weight_ref[s * 16:(s + 1) * 16, p * TILE:(p + 1) * TILE] = plane_ref[s, SUB + p * 16:SUB + (p + 1) * 16, :]


def local(features, weight, cotangent, tile_slot, tile_count, tile_edges, deg_dst, deg_src):
    bf16 = jnp.bfloat16
    shape = jax.ShapeDtypeStruct
    zh, core, zl = lax.axis_index("zh"), lax.axis_index("c"), lax.axis_index("zl")

    piece, src_scale = call(
        prepare,
        (shape((208, TILE), bf16), shape((SUB, 1), jnp.float32)),
        [SMEM, HBM, HBM, HBM, HBM],
        [
            pltpu.VMEM((SUB, TILE), bf16),
            pltpu.VMEM((1, SUB), jnp.int32),
            pltpu.VMEM((1, SLOTS), jnp.int32),
            pltpu.VMEM((SLOTS, 512), jnp.int32),
            pltpu.SemaphoreType.DMA((4,)),
        ],
        micros=1,
        name="prepare",
        limit=62,
    )(tile_count, features, deg_src[None], tile_slot, tile_edges)
    code = call(
        mark_edges,
        shape((SLOTS + 8, 512), jnp.int32),
        [SMEM, VMEM, VMEM],
        micros=1,
        name="mark_edges",
    )(tile_count, tile_slot, tile_edges)
    ring_piece = lax.all_gather(piece, "zh")
    codes = lax.all_gather(code, "c")
    slots = codes[:, SLOTS, :TILE]

    copies = call(
        fan_out,
        shape((16, 4, SUB, TILE), bf16),
        [VMEM],
        [pltpu.SemaphoreType.DMA((16,))],
        micros=1,
        name="fan_out",
        out_spec=HBM,
    )(ring_piece)
    plane_sources = lax.all_to_all(copies, ("x", "y"), 0, 0)
    tiles, dst_scale = call(
        build_forward,
        (shape((2, TILE, SLOTS * SUB), bf16), shape((NB, 1), jnp.float32)),
        [SMEM, SMEM, VMEM, VMEM],
        micros=6,
        name="build_forward",
    )(slots, core[None], codes, deg_dst[None])
    plane_sources, tiles = lax.optimization_barrier((plane_sources, tiles))

    own_sum, other_sum = call(
        aggregate,
        (shape((NB, TILE), jnp.float32), shape((NB, TILE), jnp.float32)),
        [SMEM, SMEM, VMEM, VMEM],
        [pltpu.VMEM((2, SLOTS * SUB, 2 * TILE), bf16)],
        name="aggregate",
    )(slots, core[None], tiles, plane_sources.reshape(64 * SUB, TILE))
    aggregated = call(combine, shape((4, SUB, TILE), bf16), [SMEM, VMEM, VMEM, VMEM], micros=1, name="combine")(
        core[None], own_sum, lax.all_gather(other_sum, "c"), dst_scale
    )

    panels = lax.all_to_all(aggregated, "zl", 0, 0)
    activated, spread, terms = call(
        dense,
        (shape((SUB, 512), bf16), shape((4, SUB, TILE), bf16), shape((512, 512), bf16)),
        [SMEM] + [VMEM] * 4,
        name="dense",
    )(zl[None], panels, weight, cotangent, deg_dst.reshape(4, SUB))

    parts = lax.all_to_all(terms.reshape(32, 16, 512), PLANE, 0, 0)
    adjacent = call(
        build_backward,
        shape((2048, 1024), bf16),
        [SMEM, SMEM, VMEM],
        [pltpu.SMEM((4 * SLOTS + 8,), jnp.int32), pltpu.VMEM((4 * TILE, TILE), jnp.int32)],
        micros=6,
        name="build_backward",
    )(ring_piece[:, 192, :SLOTS].astype(jnp.int32).reshape(4 * SLOTS), zh[None], ring_piece)
    parts, adjacent = lax.optimization_barrier((parts, adjacent))
    panels = call(pack_panels, shape((4, TILE, TILE), bf16), [VMEM] * 2, micros=1, name="pack_panels")(parts, spread)
    panels = lax.all_to_all(panels, "zl", 0, 0)
    merged = call(merge_panels, shape((NB + SUB, TILE), bf16), [VMEM], micros=1, name="merge_panels")(panels)
    ring = lax.all_gather(merged, "zh")
    plane = call(
        spread_back,
        shape((32, 96, TILE), bf16),
        [VMEM] * 2,
        [pltpu.VMEM((1024, TILE), bf16)],
        name="spread_back",
    )(adjacent, ring)
    plane = lax.all_to_all(plane, PLANE, 0, 0)
    feature_grad, half = call(
        finish, (shape((SUB, TILE), bf16), shape((512, 256), bf16)), [VMEM] * 2, name="finish"
    )(plane, src_scale)
    halves = lax.all_gather(half, "c")
    weight_grad = jnp.concatenate([halves[0], halves[1]], axis=1).astype(jnp.float32)
    return (activated, weight_grad, feature_grad)


def solution(mesh):
    fine = Mesh(mesh.devices.reshape([size for _, size in FINE]), [name for name, _ in FINE])
    in_specs = (
        P(ROWS, "zl"),
        P(),
        P(ROWS + ("zl",), None),
        P(ROWS, None),
        P(ROWS),
        P(ROWS, None, None),
        P(ROWS),
        P(ROWS),
    )
    out_specs = (P(ROWS + ("zl",), None), P(), P(ROWS, "zl"))
    return jax.shard_map(local, mesh=fine, in_specs=in_specs, out_specs=out_specs, check_vma=False)
```
